512 devices in a mesh: site: 32 (over z_hi, y, x), mode: 16 (over z_lo, core).
Axes of the slice: x: 4, y: 4, z: 16 (z_hi: 2, z_lo: 8; z = z_hi * 8 + z_lo), core: 2. Of those that a mesh axis runs over, the one named last changes fastest.
Arguments:
- eigvecs: bfloat16 [64, 2, 4, 3, 4, 864, 128], P('mode', None, None, None, None, 'site'), may hold values from -1.59375 to 1.59375
- eigenvalues: float32 [64], P('mode'), may hold values from 0.5 to 4
- block_map: int32 [864], P('site'), may hold values from 0 to 863, each once
- momenta: int32 [27, 3], replicated, may hold values from -2 to 2
Outputs:
- loop_field: float32 [2, 16, 4, 864, 128], P(None, 'mode', None, 'site')
- loop_momentum: float32 [2, 16, 4, 27], replicated
The draws below stay inside these ranges and needn't reach their ends.
Inputs may be any that keep to these rules, and one draw needn't show every extreme that they name: block_map names every spatial block once.
All inputs are finite; a program needn't handle non-finite values.
Results may differ from the reference program's by a relative error of at most 0.0003.
Values sent between devices are 32-bit elements; how exact they have to be, the bound alone decides.
A program may use at most 64 MiB of HBM per device.

```python
import math
import jax
import jax.numpy as jnp
import numpy as np
from jax import lax

L = 48
NMOM = 27
T_WIN = 4
MODES = 64
BLOCKS = 864


def plant(result, stream_key, least, top_value):
    longest = result.shape.index(max(result.shape))
    spots = []
    for shift in (0, 1):
        where = [jax.random.randint(jax.random.fold_in(stream_key, axis), (), 0, length) for axis, length in enumerate(result.shape)]
        where[longest] = (where[longest] + shift) % result.shape[longest]
        spots.append(tuple(where))
    return result.at[spots[0]].set(least).at[spots[1]].set(top_value)


def block_levels(key, extent, cuts, low, high):
    loudness = 1.0
    for position, blocks in cuts:
        steps = jax.random.uniform(jax.random.fold_in(jax.random.fold_in(key, 6), position), (blocks,), jnp.float32, low / len(cuts), high / len(cuts))
        loudness = loudness * jnp.repeat(jnp.exp(steps), extent[position] // blocks).reshape((-1,) + (1,) * (len(extent) - 1 - position))
    return loudness


def gaussian(stream_key, shape, deviation, most, pieces=(), kind=jnp.bfloat16):
    entries = jax.random.normal(stream_key, shape, jnp.float32) * deviation
    if len(pieces) > 0:
        entries = block_levels(stream_key, shape, pieces, -0.22, 0.18) * entries
    return jnp.clip(entries, min=-most, max=most).astype(kind)


def setup_inputs(seed: int = 0) -> dict:
    seeds = jax.random.split(jax.random.key(seed), 5)
    eigvecs = gaussian(seeds[0], (MODES, 2, 4, 3, T_WIN, BLOCKS, 128), 0.2, 1.59375, ((0, 16), (5, 32)))
    eigenvalues = jnp.clip(jnp.exp(math.log(4.0) - 2.0794415 * jax.random.uniform(seeds[1], (MODES,), jnp.float32) ** block_levels(seeds[1], (MODES,), ((0, 16),), -0.2, 0.2)), 0.5, 4.0)
    block_map = jax.random.permutation(seeds[2], BLOCKS).astype(jnp.int32)
    momenta = plant(jax.random.randint(seeds[3], (NMOM, 3), -2, 3), jax.random.fold_in(seeds[3], 1), -2, 2).astype(jnp.int32)
    return {"eigvecs": eigvecs, "eigenvalues": eigenvalues, "block_map": block_map, "momenta": momenta}


def gamma_table():
    unit = 1j
    first = np.array([[0, 0, 0, unit], [0, 0, unit, 0], [0, -unit, 0, 0], [-unit, 0, 0, 0]])
    second = np.array([[0, 0, 0, -1], [0, 0, 1, 0], [0, 1, 0, 0], [-1, 0, 0, 0]], dtype=complex)
    third = np.array([[0, 0, unit, 0], [0, 0, 0, -unit], [-unit, 0, 0, 0], [0, unit, 0, 0]])
    fourth = np.array([[0, 0, 1, 0], [0, 0, 0, 1], [1, 0, 0, 0], [0, 1, 0, 0]], dtype=complex)
    basis = [first, second, third, fourth]
    fifth = first @ second @ third @ fourth
    table = np.zeros((32, 32))
    for number in range(16):
        matrix = np.eye(4, dtype=complex)
        for bit in range(4):
            if (number >> bit) & 1:
                matrix = matrix @ basis[bit]
        matrix = matrix @ fifth
        flat_real = matrix.real.reshape(16)
        flat_imag = matrix.imag.reshape(16)
        table[number, :16] = flat_real
        table[number, 16:] = -flat_imag
        table[16 + number, :16] = flat_imag
        table[16 + number, 16:] = flat_real
    return table


def phase_tables(blocks, momenta, length):
    nby = length // 4
    nbz = length // 8
    inside = jnp.arange(128, dtype=jnp.int32)
    coord_x = 4 * (blocks // (nby * nbz))[:, None] + (inside // 32)[None, :]
    coord_y = 4 * ((blocks // nbz) % nby)[:, None] + ((inside // 8) % 4)[None, :]
    coord_z = 8 * (blocks % nbz)[:, None] + (inside % 8)[None, :]
    coord_x = coord_x.reshape(-1)
    coord_y = coord_y.reshape(-1)
    coord_z = coord_z.reshape(-1)
    products = coord_x[:, None] * momenta[None, :, 0] + coord_y[:, None] * momenta[None, :, 1] + coord_z[:, None] * momenta[None, :, 2]
    wrapped = jnp.mod(products, length).astype(jnp.int32)
    angle = wrapped.astype(jnp.float32) * jnp.float32(2.0 * math.pi / length)
    return jnp.cos(angle), jnp.sin(angle)


def project(field, cosine, sine, length):
    hp = lax.Precision.HIGHEST
    real_part = field[0]
    imag_part = field[1]
    out_real = jnp.einsum("gtx,xk->gtk", real_part, cosine, precision=hp) + jnp.einsum("gtx,xk->gtk", imag_part, sine, precision=hp)
    out_imag = jnp.einsum("gtx,xk->gtk", imag_part, cosine, precision=hp) - jnp.einsum("gtx,xk->gtk", real_part, sine, precision=hp)
    return jnp.stack([out_real, out_imag]) * jnp.float32(length ** -1.5)


def reference(eigvecs, eigenvalues, block_map, momenta):
    hp = lax.Precision.HIGHEST
    count = T_WIN * BLOCKS * 128
    weights = 1.0 / eigenvalues

    def accumulate(carry, item):
        vector, weight = item
        values = vector.astype(jnp.float32).reshape(2, 4, 3, count)
        real_part = values[0]
        imag_part = values[1]
        same = jnp.einsum("acx,bcx->abx", real_part, real_part, precision=hp) + jnp.einsum("acx,bcx->abx", imag_part, imag_part, precision=hp)
        cross = jnp.einsum("acx,bcx->abx", real_part, imag_part, precision=hp) - jnp.einsum("acx,bcx->abx", imag_part, real_part, precision=hp)
        return (carry[0] + weight * same, carry[1] + weight * cross), None

    start = (jnp.zeros((4, 4, count), jnp.float32), jnp.zeros((4, 4, count), jnp.float32))
    (dens_real, dens_imag), unused = lax.scan(accumulate, start, (eigvecs, weights))
    flat = jnp.concatenate([dens_real.reshape(16, count), dens_imag.reshape(16, count)], axis=0)
    table = jnp.asarray(gamma_table(), jnp.float32)
    field = jnp.einsum("nk,kx->nx", table, flat, precision=hp).reshape(2, 16, T_WIN, BLOCKS * 128)
    cosine, sine = phase_tables(block_map, momenta, L)
    loop_momentum = project(field, cosine, sine, L)
    return field.reshape(2, 16, T_WIN, BLOCKS, 128), loop_momentum
```

```python
import math

import jax
import jax.numpy as jnp
import numpy as np
from jax import lax
from jax.experimental import pallas as pl
from jax.experimental.pallas import tpu as pltpu
from jax.sharding import PartitionSpec as P

MESH = pl.DeviceIdType.MESH

L = 48


def gamma_table():
    unit = 1j
    first = np.array([[0, 0, 0, unit], [0, 0, unit, 0], [0, -unit, 0, 0], [-unit, 0, 0, 0]])
    second = np.array([[0, 0, 0, -1], [0, 0, 1, 0], [0, 1, 0, 0], [-1, 0, 0, 0]], dtype=complex)
    third = np.array([[0, 0, unit, 0], [0, 0, 0, -unit], [-unit, 0, 0, 0], [0, unit, 0, 0]])
    fourth = np.array([[0, 0, 1, 0], [0, 0, 0, 1], [1, 0, 0, 0], [0, 1, 0, 0]], dtype=complex)
    basis = [first, second, third, fourth]
    fifth = first @ second @ third @ fourth
    table = np.zeros((32, 32))
    for number in range(16):
        matrix = np.eye(4, dtype=complex)
        for bit in range(4):
            if number >> bit & 1:
                matrix = matrix @ basis[bit]
        matrix = matrix @ fifth
        flat_real = matrix.real.reshape(16)
        flat_imag = matrix.imag.reshape(16)
        table[number, :16] = flat_real
        table[number, 16:] = -flat_imag
        table[16 + number, :16] = flat_imag
        table[16 + number, 16:] = flat_real
    return table


def phase_tables(blocks, momenta, length):
    nby = length // 4
    nbz = length // 8
    inside = jnp.arange(128, dtype=jnp.int32)
    coord_x = 4 * (blocks // (nby * nbz))[:, None] + (inside // 32)[None, :]
    coord_y = 4 * (blocks // nbz % nby)[:, None] + (inside // 8 % 4)[None, :]
    coord_z = 8 * (blocks % nbz)[:, None] + (inside % 8)[None, :]
    coord_x = coord_x.reshape(-1)
    coord_y = coord_y.reshape(-1)
    coord_z = coord_z.reshape(-1)
    products = (
        coord_x[:, None] * momenta[None, :, 0]
        + coord_y[:, None] * momenta[None, :, 1]
        + coord_z[:, None] * momenta[None, :, 2]
    )
    wrapped = jnp.mod(products, length)
    angle = wrapped.astype(jnp.float32) * jnp.float32(2.0 * math.pi / length)
    return (jnp.cos(angle), jnp.sin(angle))


def project(field, cosine, sine, length):
    hp = lax.Precision.HIGHEST
    real_part = field[0]
    imag_part = field[1]
    out_real = jnp.einsum("gtx,xk->gtk", real_part, cosine, precision=hp) + jnp.einsum(
        "gtx,xk->gtk", imag_part, sine, precision=hp
    )
    out_imag = jnp.einsum("gtx,xk->gtk", imag_part, cosine, precision=hp) - jnp.einsum(
        "gtx,xk->gtk", real_part, sine, precision=hp
    )
    return jnp.stack([out_real, out_imag]) * jnp.float32(length ** (-1.5))


def along_z(site, mode, step):
    z = site // 16 * 8 + mode // 2
    to = lax.rem(z + step + 16, 16)
    return (to // 8 * 16 + site % 16, to % 8 * 2 + mode % 2)


def relay(x_ref, o_ref, got, token, send, recv):
    site, mode = lax.axis_index("site"), lax.axis_index("mode")
    near = pltpu.get_barrier_semaphore()
    for step in (1, -1):
        pl.semaphore_signal(near, inc=1, device_id=along_z(site, mode, step), device_id_type=MESH)
    pl.semaphore_wait(near, 2)
    for slot, step in enumerate((1, -1)):
        pl.semaphore_signal(token.at[slot], inc=1, device_id=along_z(site, mode, step), device_id_type=MESH)
    for slot in range(2):
        pl.semaphore_wait(token.at[slot], 1)
    copy = pltpu.make_async_remote_copy(
        src_ref=x_ref, dst_ref=got, send_sem=send, recv_sem=recv,
        device_id=along_z(site, mode, 2), device_id_type=MESH,
    )
    copy.start()
    copy.wait()
    o_ref[...] = got[...]


def shift(x):
    return pl.pallas_call(
        relay,
        out_shape=jax.ShapeDtypeStruct((8, 128), jnp.float32),
        in_specs=[pl.BlockSpec(memory_space=pltpu.VMEM)],
        out_specs=pl.BlockSpec(memory_space=pltpu.VMEM),
        scratch_shapes=[
            pltpu.VMEM((8, 128), jnp.float32),
            pltpu.SemaphoreType.REGULAR((2,)),
            pltpu.SemaphoreType.DMA,
            pltpu.SemaphoreType.DMA,
        ],
        compiler_params=pltpu.CompilerParams(collective_id=0, has_side_effects=True),
    )(x)


def shards(eigvecs, eigenvalues, block_map, momenta):
    hp = lax.Precision.HIGHEST
    local_modes = eigvecs.shape[0]
    slices = eigvecs.shape[4]
    slots = eigvecs.shape[5]
    count = slices * slots * 128
    weights = 1.0 / eigenvalues
    values = eigvecs.reshape(local_modes, 2, 4, 3, count)
    f32 = jnp.float32
    same = jnp.zeros((local_modes, 16, count), f32)
    cross = jnp.zeros((local_modes, 16, count), f32)
    for colour in range(3):
        real_col = values[:, 0, :, colour, :].astype(f32)
        imag_col = values[:, 1, :, colour, :].astype(f32)
        same = same + (
            real_col[:, :, None, :] * real_col[:, None, :, :]
            + imag_col[:, :, None, :] * imag_col[:, None, :, :]
        ).reshape(local_modes, 16, count)
        cross = cross + (
            real_col[:, :, None, :] * imag_col[:, None, :, :]
            - imag_col[:, :, None, :] * real_col[:, None, :, :]
        ).reshape(local_modes, 16, count)
    dens_real = jnp.sum(weights[:, None, None] * same, axis=0).reshape(4, 4, count)
    dens_imag = jnp.sum(weights[:, None, None] * cross, axis=0).reshape(4, 4, count)
    flat = jnp.concatenate([dens_real.reshape(16, count), dens_imag.reshape(16, count)], axis=0)
    table = jnp.asarray(gamma_table(), jnp.float32)
    partial_field = jnp.einsum("nk,kx->nx", table, flat, precision=hp).reshape(
        2, 16, slices, slots, 128
    )
    per_device = 16 // lax.axis_size("mode")
    offset = lax.axis_index("mode") * per_device
    summed = lax.psum(partial_field, "mode")
    share = lax.dynamic_slice_in_dim(summed, offset, per_device, 1)
    cosine, sine = phase_tables(block_map, momenta, L)
    own = project(share.reshape(2, per_device, slices, slots * 128), cosine, sine, L)
    padded = jnp.zeros((2, 16, slices, own.shape[3]), jnp.float32)
    padded = lax.dynamic_update_slice_in_dim(padded, own, offset, 1)
    flat_own = jnp.zeros((8, 128), jnp.float32) + momenta[0, 0].astype(jnp.float32)
    moved = shift(flat_own)
    padded = jnp.where(moved[0, 0] == flat_own[0, 0], padded, 0.0)
    loop_momentum = lax.psum(padded, ("site", "mode"))
    return (share, loop_momentum)


def solution(mesh):
    placed = (P("mode", None, None, None, None, "site", None), P("mode"), P("site"), P())
    return jax.shard_map(
        shards,
        mesh=mesh,
        in_specs=placed,
        out_specs=(P(None, "mode", None, "site", None), P()),
        check_vma=False,
    )
```

```python
import math

import jax
import jax.numpy as jnp
import numpy as np
from jax import lax
from jax.experimental import pallas as pl
from jax.experimental.pallas import tpu as pltpu
from jax.sharding import PartitionSpec as P

MESH = pl.DeviceIdType.MESH
F32 = jnp.float32
L = 48
LINE = 8
ROWS = 108
PAD = 112
CUTS = ((0, 64), (64, 48))
ORDER = (7, 6, 0, 1, 5, 4, 3, 2)
EARLY = 4

TREE = {
    7: {0: 2, 1: 2, 2: 7, 3: 4, 4: 7, 5: 7, 6: 7},
    6: {0: 2, 1: 2, 2: 6, 3: 4, 4: 6, 5: 6},
    5: {0: 1, 1: 5, 2: 3, 3: 5, 4: 5},
    4: {0: 1, 1: 4, 2: 3, 3: 4},
    3: {0: 1, 1: 3, 2: 3},
    2: {0: 1, 1: 2},
    1: {0: 1},
}
SLOTS = 4


def children(owner, place):
    return sorted(k for k, to in TREE[owner].items() if to == place)


def pick(index, values):
    out = jnp.int32(values[0])
    for i in range(1, len(values)):
        if values[i] != values[0]:
            out = jnp.where(index == i, jnp.int32(values[i]), out)
    return out


def gammas():
    u = 1j
    first = np.array([[0, 0, 0, u], [0, 0, u, 0], [0, -u, 0, 0], [-u, 0, 0, 0]])
    second = np.array([[0, 0, 0, -1], [0, 0, 1, 0], [0, 1, 0, 0], [-1, 0, 0, 0]], dtype=complex)
    third = np.array([[0, 0, u, 0], [0, 0, 0, -u], [-u, 0, 0, 0], [0, u, 0, 0]])
    fourth = np.array([[0, 0, 1, 0], [0, 0, 0, 1], [1, 0, 0, 0], [0, 1, 0, 0]], dtype=complex)
    basis = [first, second, third, fourth]
    fifth = first @ second @ third @ fourth
    out = []
    for number in range(16):
        matrix = np.eye(4, dtype=complex)
        for bit in range(4):
            if number >> bit & 1:
                matrix = matrix @ basis[bit]
        out.append(matrix @ fifth)
    return out


def traces():
    out = []
    for matrix in gammas():
        terms = []
        for s in range(4):
            if matrix[s, s] != 0:
                terms.append((matrix[s, s], ("d", s, s)))
            for r in range(s + 1, 4):
                real, imag = matrix[s, r] + matrix[r, s], 1j * (matrix[s, r] - matrix[r, s])
                if real != 0:
                    terms.append((real, ("a", s, r)))
                if imag != 0:
                    terms.append((imag, ("b", s, r)))
        imaginary = all(c.real == 0 for c, _ in terms)
        values = [(c.imag if imaginary else c.real, name) for c, name in terms]
        out.append((imaginary, [(c > 0, abs(c) == 2, name) for c, name in values]))
    return out


TRACES = traces()


def cosine(index):
    turn = index - 48.0 * jnp.floor(index * (1.0 / 48.0) + 0.5)
    x = (12.0 - jnp.abs(turn)) * (math.pi / 24.0)
    y = x * x
    p = -1.0 / 39916800.0
    for c in (1.0 / 362880.0, -1.0 / 5040.0, 1.0 / 120.0, -1.0 / 6.0, 1.0):
        p = p * y + c
    return x * p


def kernel(
    ev, eig, bmap, mom, field_out, mom_out,
    buf, part, other, held, wide, narrow, phase, lanes, own_p, plane, line, both,
    load_sem, core_send, core_recv, tree_send, tree_recv, mom_send, mom_recv, greet,
):
    site, mode = lax.axis_index("site"), lax.axis_index("mode")
    place, core = mode // 2, mode % 2
    half, xy = site // 16, site % 16
    x, y = xy % 4, xy // 4
    height = half * LINE + place

    def at_z(step):
        z = lax.rem(height + step + 16, 16)
        return (z // LINE * 16 + xy, z % LINE * 2 + core)

    def at_plane(column):
        return (half * 16 + column, mode)

    def in_row(step):
        return at_plane(y * 4 + lax.rem(x + step, 4))

    def in_column(step):
        return at_plane(lax.rem(y + step, 4) * 4 + x)

    def signal(sem, device):
        pl.semaphore_signal(sem, inc=1, device_id=device, device_id_type=MESH)

    twin = (site, place * 2 + 1 - core)
    barrier = pltpu.get_barrier_semaphore()
    near = [twin] + [at_z(s) for s in (1, -1, 2, -2)] + [f(s) for f in (in_row, in_column) for s in (1, 2, 3)]
    for device in near:
        signal(barrier, device)

    loads = [
        pltpu.make_async_copy(ev.at[pl.ds(24 * m, 24)], buf.at[pl.ds(24 * m, 24)], load_sem.at[m]) for m in range(4)
    ]
    for copy in loads:
        copy.start()

    lanes[...] = jnp.zeros((8, 128), jnp.int32)
    lanes[0:3, 0:27] = mom[...]
    spread = lanes[...].astype(F32)
    spread = spread + pltpu.roll(spread, 32, 1)
    spread = spread + pltpu.roll(spread, 64, 1)
    along = [jnp.broadcast_to(spread[i : i + 1], (8, 128)) for i in range(3)]
    lane = lax.broadcasted_iota(jnp.int32, (8, 128), 1)
    row = lax.broadcasted_iota(jnp.int32, (8, 128), 0)
    quarter = jnp.where(lane < 32, 0.0, jnp.where(lane < 64, -12.0, jnp.where(lane < 96, 12.0, 0.0)))
    inner = along[2] * row.astype(F32) + quarter
    for i in range(16):
        values = cosine(inner + along[1] * float(i % 4) + along[0] * float(i // 4))
        top = values.astype(jnp.bfloat16).astype(F32)
        lanes_f = (values - top)
        wide[8 * i : 8 * i + 8] = top
        narrow[8 * i : 8 * i + 8] = lanes_f
    turn = jnp.where(lane < 64, 0.0, -12.0)
    upper = row < 4
    for i in range(14):
        one, two = bmap[2 * i], bmap[min(2 * i + 1, 26)]
        def both_rows(f):
            return jnp.where(upper, f(one), f(two)).astype(F32)
        angle = along[0] * both_rows(lambda q: 4 * (q // 72)) + along[1] * both_rows(lambda q: 4 * (q // 6 % 12))
        angle = angle + along[2] * both_rows(lambda q: 8 * (q % 6))
        phase[8 * i : 8 * i + 8] = cosine(angle + turn)
    weights = [1.0 / jnp.full((8, 128), eig[m], F32) for m in range(4)]
    for par in range(2):
        for q in range(8):
            part[par, q, 104:112] = jnp.zeros((8, 128), F32)

    def density(early, rows, load):
        pairs = ((0, 3), (1, 2)) if early else ((0, 1), (2, 3), (0, 2), (1, 3))
        names = [("d", s, s) for s in range(4)] if early else []
        names += [(kind, s, r) for s, r in pairs for kind in ("a", "b")]
        total = {}
        for m in range(4):
            weight = jnp.broadcast_to(weights[m][0:1], (rows, 128))
            inside = {}
            for c in range(3):
                real = [load(m * 24 + s * 3 + c) for s in range(4)]
                imag = [load(m * 24 + 12 + s * 3 + c) for s in range(4)]
                for kind, s, r in names:
                    if kind == "b":
                        value = real[s] * imag[r] - imag[s] * real[r]
                    else:
                        value = real[s] * real[r] + imag[s] * imag[r]
                    key = (kind, s, r)
                    inside[key] = inside[key] + value if c else value
            for key in names:
                value = weight * inside[key]
                total[key] = total[key] + value if m else value
        out = []
        for q in range(EARLY) if early else range(EARLY, 8):
            for par in range(2):
                terms = TRACES[2 * ORDER[q] + par][1]
                value = None
                for positive, _, name in terms:
                    if value is None:
                        value = total[name] if positive else -total[name]
                    else:
                        value = value + total[name] if positive else value - total[name]
                if terms[0][1]:
                    value = value + value
                out.append((par, q, value))
        return out

    def groups(early, first, last):
        def body(g, carry):
            base = pl.multiple_of(g * 16, 16)
            for par, q, value in density(early, 16, lambda p: buf[p, pl.ds(base, 16)].astype(F32)):
                part[par, q, pl.ds(base, 16)] = value
            return carry
        lax.fori_loop(first, last, body, 0)

    def tail(early):
        for par, q, value in density(early, 12, lambda p: buf[p, 96:108].astype(F32)):
            part[par, q, 96:108] = value

    def to_twin(stage, cut):
        start, size = CUTS[cut]
        return pltpu.make_async_remote_copy(
            src_ref=part.at[1 - core, pl.ds(4 * stage, 4), pl.ds(start, size)],
            dst_ref=other.at[pl.ds(4 * stage, 4), pl.ds(start, size)],
            send_sem=core_send.at[stage, cut], recv_sem=core_recv.at[stage, cut],
            device_id=twin, device_id_type=MESH,
        )

    def from_twin(stage, cut):
        to_twin(stage, cut).wait_recv()
        start, size = CUTS[cut]
        for q in range(4 * stage, 4 * stage + 4):
            part[core, q, start : start + size] += other[q, start : start + size]

    ways = (place, LINE - 1 - place)

    def owner_at(way, owner):
        return ORDER.index(owner if way == 0 else LINE - 1 - owner)

    def step_to(way, owner, cut, source):
        here = ways[way]
        parents = [TREE[owner].get(k, owner) for k in range(LINE)]
        slots = [children(owner, TREE[owner][k]).index(k) if k in TREE[owner] else 0 for k in range(LINE)]
        to = pick(here, parents)
        target = to if way == 0 else LINE - 1 - to
        start, size = CUTS[cut]
        slot = pick(here, slots)
        return pltpu.make_async_remote_copy(
            src_ref=source.at[pl.ds(start, size)],
            dst_ref=held.at[way, owner, slot, pl.ds(start, size)],
            send_sem=tree_send.at[way, owner], recv_sem=tree_recv.at[way, owner, slot, cut],
            device_id=(site, target * 2 + core), device_id_type=MESH,
        )

    def arrived(way, owner, slot, cut):
        start, size = CUTS[cut]
        ref = held.at[way, owner, slot, pl.ds(start, size)]
        pltpu.make_async_remote_copy(
            src_ref=ref, dst_ref=ref, send_sem=tree_send.at[way, owner], recv_sem=tree_recv.at[way, owner, slot, cut],
            device_id=twin, device_id_type=MESH,
        ).wait_recv()

    def leaves(way, owner):
        here = ways[way]
        return pick(here, [int(k < owner and not children(owner, k)) for k in range(LINE)]) == 1

    def collectors(way, owner):
        here = ways[way]
        return [(n, pick(here, [int(k < owner and len(children(owner, k)) > n) for k in range(LINE)]) == 1)
                for n in range(max(len(children(owner, k)) for k in range(owner)))]

    def send_leaves(owner, cut):
        for way in range(2):
            @pl.when(leaves(way, owner))
            def _():
                step_to(way, owner, cut, part.at[core, owner_at(way, owner)]).start()

    def send_collected(owner, cut):
        start, size = CUTS[cut]
        for way in range(2):
            slots = collectors(way, owner)
            if not slots:
                continue

            @pl.when(slots[0][1])
            def _():
                for n, here in slots:
                    if n == 0:
                        arrived(way, owner, 0, cut)
                        held[way, owner, 0, start : start + size] += part[core, owner_at(way, owner), start : start + size]
                    else:
                        @pl.when(here)
                        def _():
                            arrived(way, owner, n, cut)
                            held[way, owner, 0, start : start + size] += held[way, owner, n, start : start + size]
                step_to(way, owner, cut, held.at[way, owner, 0]).start()

    for copy in loads:
        copy.wait()
    groups(True, 0, 4)
    pl.semaphore_wait(barrier, len(near))
    for i, device in enumerate([in_column(1), in_column(2), in_column(3), at_z(2), at_z(-2)]):
        signal(greet.at[i], device)
    to_twin(0, 0).start()
    groups(True, 4, 6)
    tail(True)
    to_twin(0, 1).start()
    groups(False, 0, 4)
    to_twin(1, 0).start()
    for cut in range(2):
        from_twin(0, cut)
        for owner in (7, 6):
            send_leaves(owner, cut)
    groups(False, 4, 6)
    tail(False)
    to_twin(1, 1).start()
    for cut in range(2):
        from_twin(1, cut)
        for owner in (5, 4, 3, 2):
            send_leaves(owner, cut)
    for cut in range(2):
        send_leaves(1, cut)
    for i in range(5):
        pl.semaphore_wait(greet.at[i], 1)
    for i, device in enumerate([at_z(1), at_z(-1), at_z(4), at_z(-4)]):
        signal(greet.at[5 + i], device)

    top = wide[...].astype(jnp.bfloat16)
    rest = narrow[...].astype(jnp.bfloat16)
    doubled = jnp.concatenate([top, top], axis=0)

    def project(q, carry):
        share = part[core, q]
        high = share.astype(jnp.bfloat16)
        low = (share - high.astype(F32)).astype(jnp.bfloat16)
        value = jnp.dot(jnp.concatenate([high, low], axis=1), doubled, preferred_element_type=F32)
        value = value + jnp.dot(high, rest, preferred_element_type=F32)
        own_p[q] = (value * phase[...]).reshape(14, 8, 128).sum(axis=0)
        return carry

    lax.fori_loop(0, 8, project, 0)
    folded = []
    for q in range(8):
        value = own_p[q]
        value = value + pltpu.roll(value, 4, 0)
        folded.append(value + pltpu.roll(value, 64, 1))
    for i in range(2):
        pairs = [jnp.where(upper, folded[4 * i + 2 * j], folded[4 * i + 2 * j + 1]) for j in range(2)]
        plane[xy, 8 * i : 8 * i + 8] = jnp.where(lane < 64, pairs[0], pairs[1])

    def share_out(buffer, slot, stage, devices):
        for device in devices:
            pltpu.make_async_remote_copy(
                src_ref=buffer.at[slot], dst_ref=buffer.at[slot], send_sem=mom_send.at[stage], recv_sem=mom_recv.at[stage],
                device_id=device, device_id_type=MESH,
            ).start()

    def gathered(buffer, count, stage):
        ref = buffer.at[pl.ds(0, count)]
        return pltpu.make_async_remote_copy(
            src_ref=ref, dst_ref=ref, send_sem=mom_send.at[stage], recv_sem=mom_recv.at[stage],
            device_id=twin, device_id_type=MESH,
        )

    share_out(plane, xy, 0, [at_plane(lax.rem(xy + s, 16)) for s in range(1, 16)])

    for owner in (7, 6):
        for cut in range(2):
            if owner == 7 and cut == 0:
                for i in (5, 6):
                    pl.semaphore_wait(greet.at[i], 1)
            send_collected(owner, cut)
    for owner in (5, 4, 3, 2):
        for cut in range(2):
            send_collected(owner, cut)

    gathered(plane, 15, 0).wait_recv()
    value = plane[0]
    for i in range(1, 16):
        value = value + plane[i]
    line[height] = value
    for i in (7, 8):
        pl.semaphore_wait(greet.at[i], 1)
    share_out(line, height, 1, [at_z(s) for s in (8, 7, -7, 6, -6, 5, -5, 4, -4, 3, -3, 2, -2, 1, -1)])

    mine = pick(place, [ORDER.index(p) for p in range(LINE)])
    for cut, (start, size) in enumerate(CUTS):
        rows = pl.ds(start, size)
        for way in range(2):
            for owner in range(1, LINE):
                count = len(children(owner, owner))
                @pl.when(ways[way] == owner)
                def _():
                    for n in range(count):
                        arrived(way, owner, n, cut)
                        part[core, mine, rows] += held[way, owner, n, start : start + size]
    total = part[core, mine]
    imaginary = pick(mode, [int(t[0]) for t in TRACES]) == 1
    field_out[0:ROWS] = jnp.where(imaginary, 0.0, total)[0:ROWS]
    field_out[ROWS : 2 * ROWS] = jnp.where(imaginary, total, 0.0)[0:ROWS]

    gathered(line, 15, 1).wait_recv()
    value = line[0]
    for i in range(1, 16):
        value = value + line[i]
    both[core] = value * (L**-1.5)
    cross = pltpu.make_async_remote_copy(
        src_ref=both.at[core], dst_ref=both.at[core], send_sem=mom_send.at[2], recv_sem=mom_recv.at[2],
        device_id=twin, device_id_type=MESH,
    )
    cross.start()

    for stage in range(2):
        for cut in range(2):
            to_twin(stage, cut).wait_send()
        gathered((plane, line)[stage], 15, stage).wait_send()
    for way in range(2):
        for owner in range(1, LINE):
            @pl.when(ways[way] < owner)
            def _():
                ref = held.at[way, owner, 0]
                pltpu.make_async_remote_copy(
                    src_ref=ref, dst_ref=ref, send_sem=tree_send.at[way, owner], recv_sem=tree_recv.at[way, owner, 0, 0],
                    device_id=twin, device_id_type=MESH,
                ).wait_send()
    cross.wait()
    for par in range(2):
        value = both[par]
        turned = [value] + [pltpu.roll(value, 128 - s, 1) for s in (32, 64, 96)]
        for q in range(8):
            n = 2 * ORDER[q] + par
            first = 8 * (q // 4) + 4 * (q % 2)
            c, s = (turned[2 * (q % 4 // 2) + j][first : first + 4, 0:27] for j in range(2))
            mom_out[0, n] = s if TRACES[n][0] else c
            mom_out[1, n] = c if TRACES[n][0] else -s


def shards(eigvecs, eigenvalues, block_map, momenta):
    vectors = eigvecs.transpose(0, 1, 2, 3, 5, 4, 6)

    def body(ev, *refs):
        kernel(ev.reshape(96, ROWS, 128), *refs)

    dma, vmem = pltpu.SemaphoreType.DMA, pltpu.VMEM
    field, sums = pl.pallas_call(
        body,
        out_shape=(jax.ShapeDtypeStruct((2 * ROWS, 128), F32), jax.ShapeDtypeStruct((2, 16, 4, 27), F32)),
        in_specs=[
            pl.BlockSpec(memory_space=pl.ANY),
            pl.BlockSpec(memory_space=pltpu.SMEM),
            pl.BlockSpec(memory_space=pltpu.SMEM),
            pl.BlockSpec(memory_space=pltpu.VMEM),
        ],
        out_specs=(pl.BlockSpec(memory_space=pltpu.VMEM), pl.BlockSpec(memory_space=pltpu.VMEM)),
        scratch_shapes=[
            vmem((96, ROWS, 128), jnp.bfloat16),
            vmem((2, 8, PAD, 128), F32),
            vmem((8, PAD, 128), F32),
            vmem((2, LINE, SLOTS, PAD, 128), F32),
            vmem((128, 128), F32),
            vmem((128, 128), F32),
            vmem((PAD, 128), F32),
            vmem((8, 128), jnp.int32),
            vmem((8, 8, 128), F32),
            vmem((16, 16, 128), F32),
            vmem((16, 16, 128), F32),
            vmem((2, 16, 128), F32),
            dma((4,)),
            dma((2, 2)),
            dma((2, 2)),
            dma((2, LINE)),
            dma((2, LINE, SLOTS, 2)),
            dma((3,)),
            dma((3,)),
            pltpu.SemaphoreType.REGULAR((9,)),
        ],
        compiler_params=pltpu.CompilerParams(collective_id=0, has_side_effects=True, vmem_limit_bytes=56 * 2**20),
        name="loops",
    )(vectors, eigenvalues, block_map, momenta.T)
    field = field.reshape(2, 1, 27, 4, 128).transpose(0, 1, 3, 2, 4)
    return field, sums


def solution(mesh):
    placed = (P("mode", None, None, None, None, "site", None), P("mode"), P("site"), P())
    return jax.shard_map(
        shards,
        mesh=mesh,
        in_specs=placed,
        out_specs=(P(None, "mode", None, "site", None), P()),
        check_vma=False,
    )
```

```python
import math

import jax
import jax.numpy as jnp
import numpy as np
from jax import lax
from jax.experimental import pallas as pl
from jax.experimental.pallas import tpu as pltpu
from jax.sharding import PartitionSpec as P

MESH = pl.DeviceIdType.MESH
F32 = jnp.float32
L = 48
LINE = 8
ROWS = 108
PAD = 112
CUTS = ((0, 64), (64, 48))
ORDER = (7, 6, 0, 1, 5, 4, 3, 2)
ROOTS = 2
EARLY = 4

TREE = {
    7: {0: 2, 1: 2, 2: 7, 3: 4, 4: 7, 5: 7, 6: 7},
    6: {0: 2, 1: 2, 2: 6, 3: 4, 4: 6, 5: 6},
    5: {0: 1, 1: 5, 2: 3, 3: 5, 4: 5},
    4: {0: 1, 1: 4, 2: 3, 3: 4},
    3: {0: 1, 1: 3, 2: 3},
    2: {0: 1, 1: 2},
    1: {0: 1},
}
SLOTS = 4


def children(owner, place):
    return sorted(k for k, to in TREE[owner].items() if to == place)


def pick(index, values):
    out = jnp.int32(values[0])
    for i in range(1, len(values)):
        if values[i] != values[0]:
            out = jnp.where(index == i, jnp.int32(values[i]), out)
    return out


def gammas():
    u = 1j
    first = np.array([[0, 0, 0, u], [0, 0, u, 0], [0, -u, 0, 0], [-u, 0, 0, 0]])
    second = np.array([[0, 0, 0, -1], [0, 0, 1, 0], [0, 1, 0, 0], [-1, 0, 0, 0]], dtype=complex)
    third = np.array([[0, 0, u, 0], [0, 0, 0, -u], [-u, 0, 0, 0], [0, u, 0, 0]])
    fourth = np.array([[0, 0, 1, 0], [0, 0, 0, 1], [1, 0, 0, 0], [0, 1, 0, 0]], dtype=complex)
    basis = [first, second, third, fourth]
    fifth = first @ second @ third @ fourth
    out = []
    for number in range(16):
        matrix = np.eye(4, dtype=complex)
        for bit in range(4):
            if number >> bit & 1:
                matrix = matrix @ basis[bit]
        out.append(matrix @ fifth)
    return out


def traces():
    out = []
    for matrix in gammas():
        terms = []
        for s in range(4):
            if matrix[s, s] != 0:
                terms.append((matrix[s, s], ("d", s, s)))
            for r in range(s + 1, 4):
                real, imag = matrix[s, r] + matrix[r, s], 1j * (matrix[s, r] - matrix[r, s])
                if real != 0:
                    terms.append((real, ("a", s, r)))
                if imag != 0:
                    terms.append((imag, ("b", s, r)))
        imaginary = all(c.real == 0 for c, _ in terms)
        values = [(c.imag if imaginary else c.real, name) for c, name in terms]
        out.append((imaginary, [(c > 0, abs(c) == 2, name) for c, name in values]))
    return out


TRACES = traces()


def cosine(index):
    turn = index - 48.0 * jnp.floor(index * (1.0 / 48.0) + 0.5)
    x = (12.0 - jnp.abs(turn)) * (math.pi / 24.0)
    y = x * x
    p = -1.0 / 39916800.0
    for c in (1.0 / 362880.0, -1.0 / 5040.0, 1.0 / 120.0, -1.0 / 6.0, 1.0):
        p = p * y + c
    return x * p


def kernel(
    ev, eig_in, bmap_in, mom_in, field_out, mom_out,
    buf, part, other, held, wide, narrow, phase, lanes, plane, line, both, eig, bmap, mom,
    load_sem, core_send, core_recv, tree_send, tree_recv, mom_send, mom_recv, greet,
):
    site, mode = lax.axis_index("site"), lax.axis_index("mode")
    place, core = mode // 2, mode % 2
    half, xy = site // 16, site % 16
    height = half * LINE + place

    def at_z(step):
        z = lax.rem(height + step + 16, 16)
        return (z // LINE * 16 + xy, z % LINE * 2 + core)

    def at_plane(column):
        return (half * 16 + column, mode)

    def signal(sem, device):
        pl.semaphore_signal(sem, inc=1, device_id=device, device_id_type=MESH)

    twin = (site, place * 2 + 1 - core)
    barrier = pltpu.get_barrier_semaphore()
    small = [
        pltpu.make_async_copy(source, target, load_sem.at[4 + i])
        for i, (source, target) in enumerate(((eig_in, eig), (bmap_in, bmap), (mom_in, mom)))
    ]
    for copy in small:
        copy.start()
    near = (1, -1, 2, -2)
    root = height < ROOTS
    signal(barrier, twin)
    for step in near:
        signal(barrier, at_z(step))
    expected = jnp.int32(1 + len(near))
    for r in range(ROOTS):
        apart = lax.rem(height - r + 16, 16)
        expected = expected + jnp.where((apart > 2) & (apart < 14), 1, 0)

    @pl.when(root)
    def _():
        for step in range(3, 14):
            signal(barrier, at_z(step))
        for step in range(1, 16):
            signal(barrier, at_plane(lax.rem(xy + step, 16)))

    expected = expected + jnp.where(root, 15, 0)

    loads = [
        pltpu.make_async_copy(ev.at[pl.ds(24 * m, 24)], buf.at[pl.ds(24 * m, 24)], load_sem.at[m]) for m in range(4)
    ]
    for copy in loads:
        copy.start()

    for copy in small:
        copy.wait()
    lanes[...] = jnp.zeros((8, 128), jnp.int32)
    lanes[0:3, 0:27] = mom[...]
    spread = lanes[...].astype(F32)
    spread = spread + pltpu.roll(spread, 32, 1)
    spread = spread + pltpu.roll(spread, 64, 1)
    along = [jnp.broadcast_to(spread[i : i + 1], (8, 128)) for i in range(3)]
    lane = lax.broadcasted_iota(jnp.int32, (8, 128), 1)
    row = lax.broadcasted_iota(jnp.int32, (8, 128), 0)
    quarter = jnp.where(lane < 32, 0.0, jnp.where(lane < 64, -12.0, jnp.where(lane < 96, 12.0, 0.0)))
    inner = along[2] * row.astype(F32) + quarter
    for i in range(16):
        values = cosine(inner + along[1] * float(i % 4) + along[0] * float(i // 4))
        top = values.astype(jnp.bfloat16).astype(F32)
        lanes_f = (values - top)
        wide[8 * i : 8 * i + 8] = top
        narrow[8 * i : 8 * i + 8] = lanes_f
    turn = jnp.where(lane < 64, 0.0, -12.0)
    upper = row < 4
    for i in range(14):
        one, two = bmap[2 * i], bmap[min(2 * i + 1, 26)]
        def both_rows(f):
            return jnp.where(upper, f(one), f(two)).astype(F32)
        angle = along[0] * both_rows(lambda q: 4 * (q // 72)) + along[1] * both_rows(lambda q: 4 * (q // 6 % 12))
        angle = angle + along[2] * both_rows(lambda q: 8 * (q % 6))
        phase[8 * i : 8 * i + 8] = cosine(angle + turn)
    weights = [1.0 / jnp.full((8, 128), eig[m], F32) for m in range(4)]
    for par in range(2):
        for q in range(8):
            part[par, q, 104:112] = jnp.zeros((8, 128), F32)

    def density(early, rows, load):
        pairs = ((0, 3), (1, 2)) if early else ((0, 1), (2, 3), (0, 2), (1, 3))
        names = [("d", s, s) for s in range(4)] if early else []
        names += [(kind, s, r) for s, r in pairs for kind in ("a", "b")]
        total = {}
        for m in range(4):
            weight = jnp.broadcast_to(weights[m][0:1], (rows, 128))
            inside = {}
            for c in range(3):
                real = [load(m * 24 + s * 3 + c) for s in range(4)]
                imag = [load(m * 24 + 12 + s * 3 + c) for s in range(4)]
                for kind, s, r in names:
                    if kind == "b":
                        value = real[s] * imag[r] - imag[s] * real[r]
                    else:
                        value = real[s] * real[r] + imag[s] * imag[r]
                    key = (kind, s, r)
                    inside[key] = inside[key] + value if c else value
            for key in names:
                value = weight * inside[key]
                total[key] = total[key] + value if m else value
        out = []
        for q in range(EARLY) if early else range(EARLY, 8):
            for par in range(2):
                terms = TRACES[2 * ORDER[q] + par][1]
                value = None
                for positive, _, name in terms:
                    if value is None:
                        value = total[name] if positive else -total[name]
                    else:
                        value = value + total[name] if positive else value - total[name]
                if terms[0][1]:
                    value = value + value
                out.append((par, q, value))
        return out

    def groups(early, first, last):
        def body(g, carry):
            base = pl.multiple_of(g * 16, 16)
            for par, q, value in density(early, 16, lambda p: buf[p, pl.ds(base, 16)].astype(F32)):
                part[par, q, pl.ds(base, 16)] = value
            return carry
        lax.fori_loop(first, last, body, 0)

    def tail(early):
        for par, q, value in density(early, 12, lambda p: buf[p, 96:108].astype(F32)):
            part[par, q, 96:108] = value

    def to_twin(stage, cut):
        start, size = CUTS[cut]
        return pltpu.make_async_remote_copy(
            src_ref=part.at[1 - core, pl.ds(4 * stage, 4), pl.ds(start, size)],
            dst_ref=other.at[pl.ds(4 * stage, 4), pl.ds(start, size)],
            send_sem=core_send.at[stage, cut], recv_sem=core_recv.at[stage, cut],
            device_id=twin, device_id_type=MESH,
        )

    def from_twin(stage, cut):
        to_twin(stage, cut).wait_recv()
        start, size = CUTS[cut]
        for q in range(4 * stage, 4 * stage + 4):
            part[core, q, start : start + size] += other[q, start : start + size]

    ways = (place, LINE - 1 - place)

    def owner_at(way, owner):
        return ORDER.index(owner if way == 0 else LINE - 1 - owner)

    def step_to(way, owner, cut, source):
        here = ways[way]
        parents = [TREE[owner].get(k, owner) for k in range(LINE)]
        slots = [children(owner, TREE[owner][k]).index(k) if k in TREE[owner] else 0 for k in range(LINE)]
        to = pick(here, parents)
        target = to if way == 0 else LINE - 1 - to
        start, size = CUTS[cut]
        slot = pick(here, slots)
        return pltpu.make_async_remote_copy(
            src_ref=source.at[pl.ds(start, size)],
            dst_ref=held.at[way, owner, slot, pl.ds(start, size)],
            send_sem=tree_send.at[way, owner], recv_sem=tree_recv.at[way, owner, slot, cut],
            device_id=(site, target * 2 + core), device_id_type=MESH,
        )

    def arrived(way, owner, slot, cut):
        start, size = CUTS[cut]
        ref = held.at[way, owner, slot, pl.ds(start, size)]
        pltpu.make_async_remote_copy(
            src_ref=ref, dst_ref=ref, send_sem=tree_send.at[way, owner], recv_sem=tree_recv.at[way, owner, slot, cut],
            device_id=twin, device_id_type=MESH,
        ).wait_recv()

    def leaves(way, owner):
        here = ways[way]
        return pick(here, [int(k < owner and not children(owner, k)) for k in range(LINE)]) == 1

    def collectors(way, owner):
        here = ways[way]
        return [(n, pick(here, [int(k < owner and len(children(owner, k)) > n) for k in range(LINE)]) == 1)
                for n in range(max(len(children(owner, k)) for k in range(owner)))]

    def send_leaves(owner, cut):
        for way in range(2):
            @pl.when(leaves(way, owner))
            def _():
                step_to(way, owner, cut, part.at[core, owner_at(way, owner)]).start()

    def send_collected(owner, cut):
        start, size = CUTS[cut]
        for way in range(2):
            slots = collectors(way, owner)
            if not slots:
                continue

            @pl.when(slots[0][1])
            def _():
                for n, here in slots:
                    if n == 0:
                        arrived(way, owner, 0, cut)
                        held[way, owner, 0, start : start + size] += part[core, owner_at(way, owner), start : start + size]
                    else:
                        @pl.when(here)
                        def _():
                            arrived(way, owner, n, cut)
                            held[way, owner, 0, start : start + size] += held[way, owner, n, start : start + size]
                step_to(way, owner, cut, held.at[way, owner, 0]).start()

    top = wide[...].astype(jnp.bfloat16)
    rest = narrow[...].astype(jnp.bfloat16)
    doubled = jnp.concatenate([top, top], axis=0)

    def project(stage):
        share = part[core, 4 * stage : 4 * stage + 4].reshape(4 * PAD, 128)
        high = share.astype(jnp.bfloat16)
        low = (share - high.astype(F32)).astype(jnp.bfloat16)
        value = jnp.dot(jnp.concatenate([high, low], axis=1), doubled, preferred_element_type=F32)
        value = value + jnp.dot(high, rest, preferred_element_type=F32)
        value = (value.reshape(4, PAD, 128) * phase[...][None]).reshape(4, 14, 8, 128).sum(axis=1)
        folded = []
        for q in range(4):
            one = value[q] + pltpu.roll(value[q], 4, 0)
            folded.append(one + pltpu.roll(one, 64, 1))
        pairs = [jnp.where(upper, folded[2 * j], folded[2 * j + 1]) for j in range(2)]
        line[height, 8 * stage : 8 * stage + 8] = jnp.where(lane < 64, pairs[0], pairs[1])

    def passed(buffer, slot, stage, device):
        return pltpu.make_async_remote_copy(
            src_ref=buffer.at[slot], dst_ref=buffer.at[slot], send_sem=mom_send.at[stage], recv_sem=mom_recv.at[stage],
            device_id=device, device_id_type=MESH,
        )

    def whole(buffer, count, stage):
        ref = buffer.at[pl.ds(0, count)]
        return pltpu.make_async_remote_copy(
            src_ref=ref, dst_ref=ref, send_sem=mom_send.at[stage], recv_sem=mom_recv.at[stage],
            device_id=twin, device_id_type=MESH,
        )

    for copy in loads:
        copy.wait()
    groups(True, 0, 4)
    pl.semaphore_wait(barrier, expected)
    for i, step in enumerate((2, -2)):
        signal(greet.at[i], at_z(step))
    to_twin(0, 0).start()
    groups(True, 4, 6)
    tail(True)
    to_twin(0, 1).start()
    groups(False, 0, 4)
    to_twin(1, 0).start()
    for cut in range(2):
        from_twin(0, cut)
        for owner in (7, 6):
            send_leaves(owner, cut)
    groups(False, 4, 6)
    tail(False)
    to_twin(1, 1).start()
    project(0)
    for cut in range(2):
        from_twin(1, cut)
    project(1)
    for r in range(ROOTS):
        @pl.when(height != r)
        def _():
            passed(line, height, 0, (xy, 2 * r + core)).start()
    for owner in (5, 4, 3, 2, 1):
        for cut in range(2):
            send_leaves(owner, cut)

    for i in range(2):
        pl.semaphore_wait(greet.at[i], 1)
    for i, step in enumerate((1, -1)):
        signal(greet.at[2 + i], at_z(step))
    for owner in (7, 6, 5, 4, 3, 2):
        for cut in range(2):
            if owner == 7 and cut == 0:
                for i in range(2):
                    pl.semaphore_wait(greet.at[2 + i], 1)
            send_collected(owner, cut)

    def added(buffer):
        value = buffer[0]
        for i in range(1, 16):
            value = value + buffer[i]
        return value

    @pl.when(root)
    def _():
        whole(line, 15, 0).wait_recv()
        plane[xy] = added(line)
        for step in range(1, 16):
            passed(plane, xy, 1, at_plane(lax.rem(xy + step, 16))).start()

    mine = pick(place, [ORDER.index(p) for p in range(LINE)])
    for cut, (start, size) in enumerate(CUTS):
        rows = pl.ds(start, size)
        for way in range(2):
            for owner in range(1, LINE):
                count = len(children(owner, owner))
                @pl.when(ways[way] == owner)
                def _():
                    for n in range(count):
                        arrived(way, owner, n, cut)
                        part[core, mine, rows] += held[way, owner, n, start : start + size]
    total = part[core, mine]
    imaginary = pick(mode, [int(t[0]) for t in TRACES]) == 1
    field_out[0:ROWS] = jnp.where(imaginary, 0.0, total)[0:ROWS]
    field_out[ROWS : 2 * ROWS] = jnp.where(imaginary, total, 0.0)[0:ROWS]

    def spread_out(start):
        for r in range(ROOTS):
            @pl.when(height == r)
            def _():
                for z in (8, 9, 10, 11, 12, 13, 14, 15) if r == 0 else (7, 6, 5, 4, 3, 2):
                    for c in range(2):
                        copy = passed(both, core, 2, (z // LINE * 16 + xy, z % LINE * 2 + c))
                        copy.start() if start else copy.wait_send()

    @pl.when(root)
    def _():
        whole(plane, 15, 1).wait_recv()
        both[core] = added(plane) * (L**-1.5)
        passed(both, core, 2, twin).start()
        spread_out(True)
        passed(both, core, 2, twin).wait_recv()

    @pl.when(jnp.logical_not(root))
    def _():
        whole(both, 2, 2).wait_recv()

    for par in range(2):
        value = both[par]
        turned = [value] + [pltpu.roll(value, 128 - s, 1) for s in (32, 64, 96)]
        for q in range(8):
            n = 2 * ORDER[q] + par
            first = 8 * (q // 4) + 4 * (q % 2)
            c, s = (turned[2 * (q % 4 // 2) + j][first : first + 4, 0:27] for j in range(2))
            mom_out[0, n] = s if TRACES[n][0] else c
            mom_out[1, n] = c if TRACES[n][0] else -s

    for stage in range(2):
        for cut in range(2):
            to_twin(stage, cut).wait_send()
    for r in range(ROOTS):
        @pl.when(height != r)
        def _():
            passed(line, height, 0, twin).wait_send()
    for way in range(2):
        for owner in range(1, LINE):
            @pl.when(ways[way] < owner)
            def _():
                ref = held.at[way, owner, 0]
                pltpu.make_async_remote_copy(
                    src_ref=ref, dst_ref=ref, send_sem=tree_send.at[way, owner], recv_sem=tree_recv.at[way, owner, 0, 0],
                    device_id=twin, device_id_type=MESH,
                ).wait_send()

    @pl.when(root)
    def _():
        whole(plane, 15, 1).wait_send()
        passed(both, core, 2, twin).wait_send()
        spread_out(False)


def deliver(field_in, mom_in, field_out, mom_out, sem):
    copies = [
        pltpu.make_async_copy(field_in, field_out, sem.at[0]),
        pltpu.make_async_copy(mom_in, mom_out, sem.at[1]),
    ]
    for copy in copies:
        copy.start()
    for copy in copies:
        copy.wait()


def shards(eigvecs, eigenvalues, block_map, momenta):
    vectors = eigvecs.transpose(0, 1, 2, 3, 5, 4, 6)

    def body(ev, *refs):
        kernel(ev.reshape(96, ROWS, 128), *refs)

    dma, vmem = pltpu.SemaphoreType.DMA, pltpu.VMEM
    anywhere = pl.BlockSpec(memory_space=pl.ANY)
    shapes = ((2 * ROWS, 128), (2, 16, 4, 27))
    field, sums = pl.pallas_call(
        body,
        out_shape=tuple(pltpu.VMEM(shape, F32) for shape in shapes),
        in_specs=[pl.BlockSpec(memory_space=pltpu.HBM)] * 4,
        out_specs=(pl.BlockSpec(memory_space=pltpu.VMEM), pl.BlockSpec(memory_space=pltpu.VMEM)),
        scratch_shapes=[
            vmem((96, ROWS, 128), jnp.bfloat16),
            vmem((2, 8, PAD, 128), F32),
            vmem((8, PAD, 128), F32),
            vmem((2, LINE, SLOTS, PAD, 128), F32),
            vmem((128, 128), F32),
            vmem((128, 128), F32),
            vmem((PAD, 128), F32),
            vmem((8, 128), jnp.int32),
            vmem((16, 16, 128), F32),
            vmem((16, 16, 128), F32),
            vmem((2, 16, 128), F32),
            pltpu.SMEM((4,), F32),
            pltpu.SMEM((27,), jnp.int32),
            vmem((3, 27), jnp.int32),
            dma((7,)),
            dma((2, 2)),
            dma((2, 2)),
            dma((2, LINE)),
            dma((2, LINE, SLOTS, 2)),
            dma((3,)),
            dma((3,)),
            pltpu.SemaphoreType.REGULAR((4,)),
        ],
        compiler_params=pltpu.CompilerParams(collective_id=0, has_side_effects=True, vmem_limit_bytes=56 * 2**20),
        name="loops",
    )(vectors, eigenvalues, block_map, momenta.T)
    field, sums = pl.pallas_call(
        deliver,
        out_shape=tuple(jax.ShapeDtypeStruct(shape, F32) for shape in shapes),
        in_specs=[pl.BlockSpec(memory_space=pltpu.VMEM)] * 2,
        out_specs=(anywhere, anywhere),
        scratch_shapes=[dma((2,))],
        name="deliver",
    )(*(pltpu.with_memory_space_constraint(a, pltpu.VMEM) for a in (field, sums)))
    field = field.reshape(2, 1, 27, 4, 128).transpose(0, 1, 3, 2, 4)
    return field, sums


def solution(mesh):
    placed = (P("mode", None, None, None, None, "site", None), P("mode"), P("site"), P())
    return jax.shard_map(
        shards,
        mesh=mesh,
        in_specs=placed,
        out_specs=(P(None, "mode", None, "site", None), P()),
        check_vma=False,
    )
```

```python
import math

import jax
import jax.numpy as jnp
import numpy as np
from jax import lax
from jax.experimental import pallas as pl
from jax.experimental.pallas import tpu as pltpu
from jax.sharding import PartitionSpec as P

MESH = pl.DeviceIdType.MESH
F32 = jnp.float32
L = 48
LINE = 8
ROWS = 108
PAD = 112
CUTS = ((0, 64), (64, 48))
ORDER = (7, 6, 0, 1, 5, 4, 3, 2)
PAIRS = tuple((s, r) for s in range(4) for r in range(s + 1, 4))
NAMES = tuple(("d", s, s) for s in range(4)) + tuple((kind, s, r) for s, r in PAIRS for kind in ("a", "b"))
ROOTS = 2

TREE = {
    7: {0: 1, 1: 7, 2: 3, 3: 7, 4: 5, 5: 7, 6: 7},
    6: {0: 1, 1: 6, 2: 3, 3: 6, 4: 5, 5: 6},
    5: {0: 1, 1: 5, 2: 3, 3: 5, 4: 5},
    4: {0: 1, 1: 4, 2: 3, 3: 4},
    3: {0: 1, 1: 3, 2: 3},
    2: {0: 1, 1: 2},
    1: {0: 1},
}
SLOTS = 4


def children(owner, place):
    return sorted(k for k, to in TREE[owner].items() if to == place)


def pick(index, values):
    out = jnp.int32(values[0])
    for i in range(1, len(values)):
        if values[i] != values[0]:
            out = jnp.where(index == i, jnp.int32(values[i]), out)
    return out


def gammas():
    u = 1j
    first = np.array([[0, 0, 0, u], [0, 0, u, 0], [0, -u, 0, 0], [-u, 0, 0, 0]])
    second = np.array([[0, 0, 0, -1], [0, 0, 1, 0], [0, 1, 0, 0], [-1, 0, 0, 0]], dtype=complex)
    third = np.array([[0, 0, u, 0], [0, 0, 0, -u], [-u, 0, 0, 0], [0, u, 0, 0]])
    fourth = np.array([[0, 0, 1, 0], [0, 0, 0, 1], [1, 0, 0, 0], [0, 1, 0, 0]], dtype=complex)
    basis = [first, second, third, fourth]
    fifth = first @ second @ third @ fourth
    out = []
    for number in range(16):
        matrix = np.eye(4, dtype=complex)
        for bit in range(4):
            if number >> bit & 1:
                matrix = matrix @ basis[bit]
        out.append(matrix @ fifth)
    return out


def traces():
    out = []
    for matrix in gammas():
        terms = []
        for s in range(4):
            if matrix[s, s] != 0:
                terms.append((matrix[s, s], ("d", s, s)))
            for r in range(s + 1, 4):
                real, imag = matrix[s, r] + matrix[r, s], 1j * (matrix[s, r] - matrix[r, s])
                if real != 0:
                    terms.append((real, ("a", s, r)))
                if imag != 0:
                    terms.append((imag, ("b", s, r)))
        imaginary = all(c.real == 0 for c, _ in terms)
        values = [(c.imag if imaginary else c.real, name) for c, name in terms]
        out.append((imaginary, [(c > 0, abs(c) == 2, name) for c, name in values]))
    return out


TRACES = traces()


def cosine(index):
    turn = index - 48.0 * jnp.floor(index * (1.0 / 48.0) + 0.5)
    x = (12.0 - jnp.abs(turn)) * (math.pi / 24.0)
    y = x * x
    p = -1.0 / 39916800.0
    for c in (1.0 / 362880.0, -1.0 / 5040.0, 1.0 / 120.0, -1.0 / 6.0, 1.0):
        p = p * y + c
    return x * p


def kernel(
    ev, eig_in, bmap_in, mom_in, field_out, mom_out,
    buf, sums, part, other, held, wide, narrow, phase, lanes, share, own, line, plane, both, eig, bmap, mom,
    load_sem, core_send, core_recv, tree_send, tree_recv, mom_send, mom_recv, greet,
):
    site, mode = lax.axis_index("site"), lax.axis_index("mode")
    place, core = mode // 2, mode % 2
    half, xy = site // 16, site % 16
    height = half * LINE + place

    def at_z(step):
        z = lax.rem(height + step + 16, 16)
        return (z // LINE * 16 + xy, z % LINE * 2 + core)

    def at_plane(column):
        return (half * 16 + column, mode)

    def signal(sem, device):
        pl.semaphore_signal(sem, inc=1, device_id=device, device_id_type=MESH)

    twin = (site, place * 2 + 1 - core)
    barrier = pltpu.get_barrier_semaphore()
    small = [
        pltpu.make_async_copy(source, target, load_sem.at[4 + i])
        for i, (source, target) in enumerate(((eig_in, eig), (bmap_in, bmap), (mom_in, mom)))
    ]
    for copy in small:
        copy.start()
    near = (1, -1, 2, -2)
    root = height < ROOTS
    signal(barrier, twin)
    for step in near:
        signal(barrier, at_z(step))
    expected = jnp.int32(1 + len(near))
    for r in range(ROOTS):
        apart = lax.rem(height - r + 16, 16)
        expected = expected + jnp.where((apart > 2) & (apart < 14), 2, jnp.where(apart == 0, 0, 1))

    @pl.when(root)
    def _():
        for step in range(3, 14):
            signal(barrier, at_z(step))
        for step in range(1, 16):
            z = lax.rem(height + step, 16)
            signal(barrier, (z // LINE * 16 + xy, z % LINE * 2 + 1 - core))
        for step in range(1, 16):
            signal(barrier, at_plane(lax.rem(xy + step, 16)))

    expected = expected + jnp.where(root, 15, 0)

    loads = [
        pltpu.make_async_copy(ev.at[pl.ds(24 * m, 24)], buf.at[pl.ds(24 * m, 24)], load_sem.at[m]) for m in range(4)
    ]
    for copy in loads:
        copy.start()

    for copy in small:
        copy.wait()
    lanes[...] = jnp.zeros((8, 128), jnp.int32)
    lanes[0:3, 0:27] = mom[...]
    spread = lanes[...].astype(F32)
    spread = spread + pltpu.roll(spread, 32, 1)
    spread = spread + pltpu.roll(spread, 64, 1)
    along = [jnp.broadcast_to(spread[i : i + 1], (8, 128)) for i in range(3)]
    lane = lax.broadcasted_iota(jnp.int32, (8, 128), 1)
    row = lax.broadcasted_iota(jnp.int32, (8, 128), 0)
    quarter = jnp.where(lane < 32, 0.0, jnp.where(lane < 64, -12.0, jnp.where(lane < 96, 12.0, 0.0)))
    inner = along[2] * row.astype(F32) + quarter
    for i in range(16):
        values = cosine(inner + along[1] * float(i % 4) + along[0] * float(i // 4))
        top = values.astype(jnp.bfloat16).astype(F32)
        lanes_f = (values - top)
        wide[8 * i : 8 * i + 8] = top
        narrow[8 * i : 8 * i + 8] = lanes_f
    turn = jnp.where(lane < 64, 0.0, -12.0)
    upper = row < 4
    for i in range(14):
        one, two = bmap[2 * i], bmap[min(2 * i + 1, 26)]
        def both_rows(f):
            return jnp.where(upper, f(one), f(two)).astype(F32)
        angle = along[0] * both_rows(lambda q: 4 * (q // 72)) + along[1] * both_rows(lambda q: 4 * (q // 6 % 12))
        angle = angle + along[2] * both_rows(lambda q: 8 * (q % 6))
        phase[8 * i : 8 * i + 8] = cosine(angle + turn)
    weights = [1.0 / jnp.full((8, 128), eig[m], F32) for m in range(4)]
    for par in range(2):
        for q in range(8):
            part[par, q, 104:112] = jnp.zeros((8, 128), F32)

    def density(modes, load):
        total = {}
        for m in modes:
            inside = {}
            for c in range(3):
                real = [load(m * 24 + s * 3 + c) for s in range(4)]
                imag = [load(m * 24 + 12 + s * 3 + c) for s in range(4)]
                for key in NAMES:
                    kind, s, r = key
                    if kind == "b":
                        value = real[s] * imag[r] - imag[s] * real[r]
                    else:
                        value = real[s] * real[r] + imag[s] * imag[r]
                    inside[key] = inside[key] + value if c else value
            for key in NAMES:
                value = weights[m][0 : inside[key].shape[0]] * inside[key]
                total[key] = total[key] + value if m != modes[0] else value
        return total

    def halves(base, size):
        for first in range(0, size, 8):
            last = min(first + 8, size)
            yield first, last - first, lambda p, i=first, j=last: buf[p, pl.ds(base, size)].astype(F32)[i:j]

    def begin(base, size):
        for first, count, load in halves(base, size):
            total = density((0, 1), load)
            for i, key in enumerate(NAMES):
                sums[i, pl.ds(base + first, count)] = total[key]

    def finish(base, size):
        for first, count, load in halves(base, size):
            total = density((2, 3), load)
            for i, key in enumerate(NAMES):
                total[key] = total[key] + sums[i, pl.ds(base + first, count)]
            for q in range(8):
                for par in range(2):
                    terms = TRACES[2 * ORDER[q] + par][1]
                    value = None
                    for positive, _, name in terms:
                        if value is None:
                            value = total[name] if positive else -total[name]
                        else:
                            value = value + total[name] if positive else value - total[name]
                    if terms[0][1]:
                        value = value + value
                    part[par, q, pl.ds(base + first, count)] = value
        rows = pl.ds(base, 16)
        field = jnp.concatenate([part[par, q, rows] for par in range(2) for q in range(8)], axis=0)
        high = field.astype(jnp.bfloat16)
        low = (field - high.astype(F32)).astype(jnp.bfloat16)
        value = jnp.dot(jnp.concatenate([high, low], axis=1), doubled, preferred_element_type=F32)
        value = value + jnp.dot(high, rest, preferred_element_type=F32)
        value = (value.reshape(16, 2, 8, 128) * phase[rows].reshape(1, 2, 8, 128)).sum(axis=1)
        share[...] += value

    def groups(what, first, last):
        def body(g, carry):
            what(pl.multiple_of(g * 16, 16), 16)
            return carry
        lax.fori_loop(first, last, body, 0)

    def to_twin(cut):
        start, size = CUTS[cut]
        return pltpu.make_async_remote_copy(
            src_ref=part.at[1 - core, :, pl.ds(start, size)], dst_ref=other.at[:, pl.ds(start, size)],
            send_sem=core_send.at[cut], recv_sem=core_recv.at[cut], device_id=twin, device_id_type=MESH,
        )

    def from_twin(cut):
        to_twin(cut).wait_recv()
        start, size = CUTS[cut]
        for q in range(8):
            part[core, q, start : start + size] += other[q, start : start + size]

    ways = (place, LINE - 1 - place)

    def owner_at(way, owner):
        return ORDER.index(owner if way == 0 else LINE - 1 - owner)

    def step_to(way, owner, cut, source):
        here = ways[way]
        parents = [TREE[owner].get(k, owner) for k in range(LINE)]
        slots = [children(owner, TREE[owner][k]).index(k) if k in TREE[owner] else 0 for k in range(LINE)]
        to = pick(here, parents)
        target = to if way == 0 else LINE - 1 - to
        start, size = CUTS[cut]
        slot = pick(here, slots)
        return pltpu.make_async_remote_copy(
            src_ref=source.at[pl.ds(start, size)],
            dst_ref=held.at[way, owner, slot, pl.ds(start, size)],
            send_sem=tree_send.at[way, owner], recv_sem=tree_recv.at[way, owner, slot, cut],
            device_id=(site, target * 2 + core), device_id_type=MESH,
        )

    def arrived(way, owner, slot, cut):
        start, size = CUTS[cut]
        ref = held.at[way, owner, slot, pl.ds(start, size)]
        pltpu.make_async_remote_copy(
            src_ref=ref, dst_ref=ref, send_sem=tree_send.at[way, owner], recv_sem=tree_recv.at[way, owner, slot, cut],
            device_id=twin, device_id_type=MESH,
        ).wait_recv()

    def leaves(way, owner):
        here = ways[way]
        return pick(here, [int(k < owner and not children(owner, k)) for k in range(LINE)]) == 1

    def collectors(way, owner):
        here = ways[way]
        return [(n, pick(here, [int(k < owner and len(children(owner, k)) > n) for k in range(LINE)]) == 1)
                for n in range(max(len(children(owner, k)) for k in range(owner)))]

    def send_leaves(owner, cut, ways_too=(1, 0)):
        for way in ways_too:
            @pl.when(leaves(way, owner))
            def _():
                step_to(way, owner, cut, part.at[core, owner_at(way, owner)]).start()

    def send_collected(owner, cut):
        start, size = CUTS[cut]
        for way in (1, 0):
            slots = collectors(way, owner)
            if not slots:
                continue

            @pl.when(slots[0][1])
            def _():
                for n, here in slots:
                    if n == 0:
                        arrived(way, owner, 0, cut)
                        held[way, owner, 0, start : start + size] += part[core, owner_at(way, owner), start : start + size]
                    else:
                        @pl.when(here)
                        def _():
                            arrived(way, owner, n, cut)
                            held[way, owner, 0, start : start + size] += held[way, owner, n, start : start + size]
                step_to(way, owner, cut, held.at[way, owner, 0]).start()

    top = wide[...].astype(jnp.bfloat16)
    rest = narrow[...].astype(jnp.bfloat16)
    doubled = jnp.concatenate([top, top], axis=0)

    def passed(source, target, stage, device):
        return pltpu.make_async_remote_copy(
            src_ref=source, dst_ref=target, send_sem=mom_send.at[stage], recv_sem=mom_recv.at[stage],
            device_id=device, device_id_type=MESH,
        )

    def whole(buffer, count, stage):
        ref = buffer.at[pl.ds(0, count)]
        return pltpu.make_async_remote_copy(
            src_ref=ref, dst_ref=ref, send_sem=mom_send.at[stage], recv_sem=mom_recv.at[stage],
            device_id=twin, device_id_type=MESH,
        )

    share[...] = jnp.zeros_like(share)
    for copy in loads[:2]:
        copy.wait()
    groups(begin, 0, 6)
    begin(96, 12)
    for copy in loads[2:]:
        copy.wait()
    pl.semaphore_wait(barrier, expected)
    for i, step in enumerate((2, -2)):
        signal(greet.at[i], at_z(step))
    groups(finish, 0, 4)
    to_twin(0).start()
    groups(finish, 4, 6)
    finish(96, 12)
    to_twin(1).start()

    slot = 2 * height + core
    for par in range(2):
        for i in range(2):
            folded = []
            for q in range(4):
                one = share[8 * par + 4 * i + q]
                one = one + pltpu.roll(one, 4, 0)
                folded.append(one + pltpu.roll(one, 64, 1))
            pairs = [jnp.where(upper, folded[2 * j], folded[2 * j + 1]) for j in range(2)]
            own[par, 8 * i : 8 * i + 8] = jnp.where(lane < 64, pairs[0], pairs[1])

    def to_root(r, par):
        return passed(own.at[par], line.at[slot], 0, (xy, 2 * r + par))

    for r in range(ROOTS):
        @pl.when(height != r)
        def _():
            for par in range(2):
                to_root(r, par).start()

    @pl.when(root)
    def _():
        passed(own.at[1 - core], line.at[slot], 0, twin).start()
        line[slot] = own[core]

    for cut in range(2):
        from_twin(cut)
        for owner in (7, 6):
            send_leaves(owner, cut)
    for owner in (5, 4, 3, 2, 1):
        for cut in range(2):
            send_leaves(owner, cut, (0,))

    for i in range(2):
        pl.semaphore_wait(greet.at[i], 1)
    for i, step in enumerate((2, -2)):
        signal(greet.at[2 + i], at_z(step))
    for i in range(2):
        pl.semaphore_wait(greet.at[2 + i], 1)
    for owner in (7, 6):
        for cut in range(2):
            send_collected(owner, cut)
    mine = pick(place, [ORDER.index(p) for p in range(LINE)])

    def take(way, owner, slots):
        for cut, (start, size) in enumerate(CUTS):
            for n in slots:
                arrived(way, owner, n, cut)
                part[core, mine, start : start + size] += held[way, owner, n, start : start + size]

    for way in range(2):
        @pl.when(ways[way] == 7)
        def _():
            take(way, 7, (3,))
    for owner in (5, 4, 3, 2, 1):
        for cut in range(2):
            send_leaves(owner, cut, (1,))

    def added(buffer, first, count):
        value = buffer[first]
        for i in range(1, count):
            value = value + buffer[first + i]
        return value

    @pl.when(root)
    def _():
        whole(line, 31, 0).wait_recv()
        plane[xy] = added(line, 0, 32)
        for step in range(1, 16):
            passed(plane.at[xy], plane.at[xy], 1, at_plane(lax.rem(xy + step, 16))).start()

    for owner in (5, 4, 3, 2):
        for cut in range(2):
            send_collected(owner, cut)

    def spread_out(start):
        for r in range(ROOTS):
            @pl.when(height == r)
            def _():
                for z in (8, 9, 10, 11, 12, 13, 14, 15) if r == 0 else (7, 6, 5, 4, 3, 2):
                    for c in range(2):
                        copy = passed(both.at[core], both.at[core], 2, (z // LINE * 16 + xy, z % LINE * 2 + c))
                        copy.start() if start else copy.wait_send()

    @pl.when(root)
    def _():
        whole(plane, 15, 1).wait_recv()
        both[core] = added(plane, 0, 16) * (L**-1.5)
        passed(both.at[core], both.at[core], 2, twin).start()
        spread_out(True)

    for way in range(2):
        for owner in range(1, LINE):
            @pl.when(ways[way] == owner)
            def _():
                take(way, owner, range(3 if owner == 7 else len(children(owner, owner))))
    total = part[core, mine]
    imaginary = pick(mode, [int(t[0]) for t in TRACES]) == 1
    field_out[0:ROWS] = jnp.where(imaginary, 0.0, total)[0:ROWS]
    field_out[ROWS : 2 * ROWS] = jnp.where(imaginary, total, 0.0)[0:ROWS]

    @pl.when(root)
    def _():
        passed(both.at[core], both.at[core], 2, twin).wait_recv()

    @pl.when(jnp.logical_not(root))
    def _():
        whole(both, 2, 2).wait_recv()

    for par in range(2):
        value = both[par]
        turned = [value] + [pltpu.roll(value, 128 - s, 1) for s in (32, 64, 96)]
        for q in range(8):
            n = 2 * ORDER[q] + par
            first = 8 * (q // 4) + 4 * (q % 2)
            c, s = (turned[2 * (q % 4 // 2) + j][first : first + 4, 0:27] for j in range(2))
            mom_out[0, n] = s if TRACES[n][0] else c
            mom_out[1, n] = c if TRACES[n][0] else -s

    for cut in range(2):
        to_twin(cut).wait_send()
    for r in range(ROOTS):
        @pl.when(height != r)
        def _():
            for par in range(2):
                to_root(r, par).wait_send()
    for way in range(2):
        for owner in range(1, LINE):
            @pl.when(ways[way] < owner)
            def _():
                ref = held.at[way, owner, 0]
                pltpu.make_async_remote_copy(
                    src_ref=ref, dst_ref=ref, send_sem=tree_send.at[way, owner], recv_sem=tree_recv.at[way, owner, 0, 0],
                    device_id=twin, device_id_type=MESH,
                ).wait_send()

    @pl.when(root)
    def _():
        passed(own.at[1 - core], line.at[slot], 0, twin).wait_send()
        whole(plane, 15, 1).wait_send()
        passed(both.at[core], both.at[core], 2, twin).wait_send()
        spread_out(False)


def deliver(field_in, mom_in, field_out, mom_out, sem):
    copies = [
        pltpu.make_async_copy(field_in, field_out, sem.at[0]),
        pltpu.make_async_copy(mom_in, mom_out, sem.at[1]),
    ]
    for copy in copies:
        copy.start()
    for copy in copies:
        copy.wait()


def shards(eigvecs, eigenvalues, block_map, momenta):
    vectors = eigvecs.transpose(0, 1, 2, 3, 5, 4, 6)

    def body(ev, *refs):
        kernel(ev.reshape(96, ROWS, 128), *refs)

    dma, vmem = pltpu.SemaphoreType.DMA, pltpu.VMEM
    anywhere = pl.BlockSpec(memory_space=pl.ANY)
    shapes = ((2 * ROWS, 128), (2, 16, 4, 27))
    field, sums = pl.pallas_call(
        body,
        out_shape=tuple(pltpu.VMEM(shape, F32) for shape in shapes),
        in_specs=[pl.BlockSpec(memory_space=pltpu.HBM)] * 4,
        out_specs=(pl.BlockSpec(memory_space=pltpu.VMEM), pl.BlockSpec(memory_space=pltpu.VMEM)),
        scratch_shapes=[
            vmem((96, ROWS, 128), jnp.bfloat16),
            vmem((16, PAD, 128), F32),
            vmem((2, 8, PAD, 128), F32),
            vmem((8, PAD, 128), F32),
            vmem((2, LINE, SLOTS, PAD, 128), F32),
            vmem((128, 128), F32),
            vmem((128, 128), F32),
            vmem((PAD, 128), F32),
            vmem((8, 128), jnp.int32),
            vmem((16, 8, 128), F32),
            vmem((2, 16, 128), F32),
            vmem((32, 16, 128), F32),
            vmem((16, 16, 128), F32),
            vmem((2, 16, 128), F32),
            pltpu.SMEM((4,), F32),
            pltpu.SMEM((27,), jnp.int32),
            vmem((3, 27), jnp.int32),
            dma((7,)),
            dma((2,)),
            dma((2,)),
            dma((2, LINE)),
            dma((2, LINE, SLOTS, 2)),
            dma((3,)),
            dma((3,)),
            pltpu.SemaphoreType.REGULAR((4,)),
        ],
        compiler_params=pltpu.CompilerParams(collective_id=0, has_side_effects=True, vmem_limit_bytes=56 * 2**20),
        name="loops",
    )(vectors, eigenvalues, block_map, momenta.T)
    field, sums = pl.pallas_call(
        deliver,
        out_shape=tuple(jax.ShapeDtypeStruct(shape, F32) for shape in shapes),
        in_specs=[pl.BlockSpec(memory_space=pltpu.VMEM)] * 2,
        out_specs=(anywhere, anywhere),
        scratch_shapes=[dma((2,))],
        name="deliver",
    )(*(pltpu.with_memory_space_constraint(a, pltpu.VMEM) for a in (field, sums)))
    field = field.reshape(2, 1, 27, 4, 128).transpose(0, 1, 3, 2, 4)
    return field, sums


def solution(mesh):
    placed = (P("mode", None, None, None, None, "site", None), P("mode"), P("site"), P())
    return jax.shard_map(
        shards,
        mesh=mesh,
        in_specs=placed,
        out_specs=(P(None, "mode", None, "site", None), P()),
        check_vma=False,
    )
```

```python
import math

import jax
import jax.numpy as jnp
import numpy as np
from jax import lax
from jax.experimental import pallas as pl
from jax.experimental.pallas import tpu as pltpu
from jax.sharding import PartitionSpec as P

MESH = pl.DeviceIdType.MESH
F32 = jnp.float32
L = 48
LINE = 8
ROWS = 108
PAD = 112
CUTS = ((0, 64), (64, 48))
ORDER = (7, 6, 0, 1, 5, 4, 3, 2)
PAIRS = tuple((s, r) for s in range(4) for r in range(s + 1, 4))
NAMES = tuple(("d", s, s) for s in range(4)) + tuple((kind, s, r) for s, r in PAIRS for kind in ("a", "b"))
ROOTS = 2

TREE = {
    7: {0: 1, 1: 7, 2: 3, 3: 7, 4: 5, 5: 7, 6: 7},
    6: {0: 1, 1: 6, 2: 3, 3: 6, 4: 5, 5: 6},
    5: {0: 1, 1: 5, 2: 3, 3: 5, 4: 5},
    4: {0: 1, 1: 4, 2: 3, 3: 4},
    3: {0: 1, 1: 3, 2: 3},
    2: {0: 1, 1: 2},
    1: {0: 1},
}
SLOTS = 4


def children(owner, place):
    return sorted(k for k, to in TREE[owner].items() if to == place)


def pick(index, values):
    out = jnp.int32(values[0])
    for i in range(1, len(values)):
        if values[i] != values[0]:
            out = jnp.where(index == i, jnp.int32(values[i]), out)
    return out


def gammas():
    u = 1j
    first = np.array([[0, 0, 0, u], [0, 0, u, 0], [0, -u, 0, 0], [-u, 0, 0, 0]])
    second = np.array([[0, 0, 0, -1], [0, 0, 1, 0], [0, 1, 0, 0], [-1, 0, 0, 0]], dtype=complex)
    third = np.array([[0, 0, u, 0], [0, 0, 0, -u], [-u, 0, 0, 0], [0, u, 0, 0]])
    fourth = np.array([[0, 0, 1, 0], [0, 0, 0, 1], [1, 0, 0, 0], [0, 1, 0, 0]], dtype=complex)
    basis = [first, second, third, fourth]
    fifth = first @ second @ third @ fourth
    out = []
    for number in range(16):
        matrix = np.eye(4, dtype=complex)
        for bit in range(4):
            if number >> bit & 1:
                matrix = matrix @ basis[bit]
        out.append(matrix @ fifth)
    return out


def traces():
    out = []
    for matrix in gammas():
        terms = []
        for s in range(4):
            if matrix[s, s] != 0:
                terms.append((matrix[s, s], ("d", s, s)))
            for r in range(s + 1, 4):
                real, imag = matrix[s, r] + matrix[r, s], 1j * (matrix[s, r] - matrix[r, s])
                if real != 0:
                    terms.append((real, ("a", s, r)))
                if imag != 0:
                    terms.append((imag, ("b", s, r)))
        imaginary = all(c.real == 0 for c, _ in terms)
        values = [(c.imag if imaginary else c.real, name) for c, name in terms]
        out.append((imaginary, [(c > 0, abs(c) == 2, name) for c, name in values]))
    return out


TRACES = traces()


def cosine(index):
    turn = index - 48.0 * jnp.floor(index * (1.0 / 48.0) + 0.5)
    x = (12.0 - jnp.abs(turn)) * (math.pi / 24.0)
    y = x * x
    p = -1.0 / 39916800.0
    for c in (1.0 / 362880.0, -1.0 / 5040.0, 1.0 / 120.0, -1.0 / 6.0, 1.0):
        p = p * y + c
    return x * p


def kernel(
    ev, eig_in, bmap_in, mom_in, field_out, mom_out,
    buf, sums, part, other, held, wide, narrow, phase, lanes, own, line, plane, both, eig, bmap, mom,
    load_sem, core_send, core_recv, tree_send, tree_recv, mom_send, mom_recv, greet,
):
    site, mode = lax.axis_index("site"), lax.axis_index("mode")
    place, core = mode // 2, mode % 2
    half, xy = site // 16, site % 16
    height = half * LINE + place

    def at_z(step):
        z = lax.rem(height + step + 16, 16)
        return (z // LINE * 16 + xy, z % LINE * 2 + core)

    def at_plane(column):
        return (half * 16 + column, mode)

    def signal(sem, device):
        pl.semaphore_signal(sem, inc=1, device_id=device, device_id_type=MESH)

    twin = (site, place * 2 + 1 - core)
    loads = [
        pltpu.make_async_copy(ev.at[pl.ds(48 * m, 48)], buf.at[pl.ds(48 * m, 48)], load_sem.at[m]) for m in range(2)
    ]
    small = [
        pltpu.make_async_copy(source, target, load_sem.at[2 + i])
        for i, (source, target) in enumerate(((eig_in, eig), (bmap_in, bmap), (mom_in, mom)))
    ]
    for copy in small + loads:
        copy.start()
    barrier = pltpu.get_barrier_semaphore()
    near = (1, -1, 2, -2)
    root = height < ROOTS
    signal(barrier, twin)
    for step in near:
        signal(barrier, at_z(step))
    expected = jnp.int32(1 + len(near))
    for r in range(ROOTS):
        apart = lax.rem(height - r + 16, 16)
        expected = expected + jnp.where((apart > 2) & (apart < 14), 2, jnp.where(apart == 0, 0, 1))

    @pl.when(root)
    def _():
        for step in range(3, 14):
            signal(barrier, at_z(step))
        for step in range(1, 16):
            z = lax.rem(height + step, 16)
            signal(barrier, (z // LINE * 16 + xy, z % LINE * 2 + 1 - core))
        for step in range(1, 16):
            signal(barrier, at_plane(lax.rem(xy + step, 16)))

    expected = expected + jnp.where(root, 15, 0)

    for copy in small:
        copy.wait()
    lanes[...] = jnp.zeros((8, 128), jnp.int32)
    lanes[0:3, 0:27] = mom[...]
    spread = lanes[...].astype(F32)
    spread = spread + pltpu.roll(spread, 32, 1)
    spread = spread + pltpu.roll(spread, 64, 1)
    along = [jnp.broadcast_to(spread[i : i + 1], (8, 128)) for i in range(3)]
    lane = lax.broadcasted_iota(jnp.int32, (8, 128), 1)
    row = lax.broadcasted_iota(jnp.int32, (8, 128), 0)
    quarter = jnp.where(lane < 32, 0.0, jnp.where(lane < 64, -12.0, jnp.where(lane < 96, 12.0, 0.0)))
    inner = along[2] * row.astype(F32) + quarter
    for i in range(16):
        values = cosine(inner + along[1] * float(i % 4) + along[0] * float(i // 4))
        top = values.astype(jnp.bfloat16).astype(F32)
        lanes_f = (values - top)
        wide[8 * i : 8 * i + 8] = top
        narrow[8 * i : 8 * i + 8] = lanes_f
    turn = jnp.where(lane < 64, 0.0, -12.0)
    upper = row < 4
    for i in range(14):
        one, two = bmap[2 * i], bmap[min(2 * i + 1, 26)]
        def both_rows(f):
            return jnp.where(upper, f(one), f(two)).astype(F32)
        angle = along[0] * both_rows(lambda q: 4 * (q // 72)) + along[1] * both_rows(lambda q: 4 * (q // 6 % 12))
        angle = angle + along[2] * both_rows(lambda q: 8 * (q % 6))
        phase[8 * i : 8 * i + 8] = cosine(angle + turn)
    weights = [1.0 / jnp.full((8, 128), eig[m], F32) for m in range(4)]
    for par in range(2):
        for q in range(8):
            part[par, q, 104:112] = jnp.zeros((8, 128), F32)

    def density(modes, load):
        total = {}
        for m in modes:
            inside = {}
            for c in range(3):
                real = [load(m * 24 + s * 3 + c) for s in range(4)]
                imag = [load(m * 24 + 12 + s * 3 + c) for s in range(4)]
                for key in NAMES:
                    kind, s, r = key
                    if kind == "b":
                        value = real[s] * imag[r] - imag[s] * real[r]
                    else:
                        value = real[s] * real[r] + imag[s] * imag[r]
                    inside[key] = inside[key] + value if c else value
            for key in NAMES:
                value = weights[m][0 : inside[key].shape[0]] * inside[key]
                total[key] = total[key] + value if m != modes[0] else value
        return total

    def halves(base, size):
        for first in range(0, size, 8):
            last = min(first + 8, size)
            yield first, last - first, lambda p, i=first, j=last: buf[p, pl.ds(base, size)].astype(F32)[i:j]

    def begin(base, size):
        for first, count, load in halves(base, size):
            total = density((0, 1), load)
            for i, key in enumerate(NAMES):
                sums[i, pl.ds(base + first, count)] = total[key]

    def finish(base, size):
        for first, count, load in halves(base, size):
            total = density((2, 3), load)
            for i, key in enumerate(NAMES):
                total[key] = total[key] + sums[i, pl.ds(base + first, count)]
            for q in range(8):
                for par in range(2):
                    terms = TRACES[2 * ORDER[q] + par][1]
                    value = None
                    for positive, _, name in terms:
                        if value is None:
                            value = total[name] if positive else -total[name]
                        else:
                            value = value + total[name] if positive else value - total[name]
                    if terms[0][1]:
                        value = value + value
                    part[par, q, pl.ds(base + first, count)] = value

    def project(start, size):
        rows = pl.ds(start, size)
        field = jnp.concatenate([part[par, q, rows] for par in range(2) for q in range(8)], axis=0)
        high = field.astype(jnp.bfloat16)
        low = (field - high.astype(F32)).astype(jnp.bfloat16)
        value = jnp.dot(jnp.concatenate([high, low], axis=1), tables, preferred_element_type=F32)
        value = value[:, 0:128] + value[:, 128:256]
        value = (value.reshape(16, size // 8, 8, 128) * phase[rows].reshape(1, size // 8, 8, 128)).sum(axis=1)
        return value

    def groups(what, first, last):
        def body(g, carry):
            what(pl.multiple_of(g * 16, 16), 16)
            return carry
        lax.fori_loop(first, last, body, 0)

    def to_twin(cut):
        start, size = CUTS[cut]
        return pltpu.make_async_remote_copy(
            src_ref=part.at[1 - core, :, pl.ds(start, size)], dst_ref=other.at[:, pl.ds(start, size)],
            send_sem=core_send.at[cut], recv_sem=core_recv.at[cut], device_id=twin, device_id_type=MESH,
        )

    def from_twin(cut):
        to_twin(cut).wait_recv()
        start, size = CUTS[cut]
        for q in range(8):
            part[core, q, start : start + size] += other[q, start : start + size]

    ways = (place, LINE - 1 - place)

    def chip(way, k):
        return k if way == 0 else LINE - 1 - k

    def routes(way, owner):
        here, tree = ways[way], TREE[owner]
        sends = [k in tree for k in range(LINE)]
        straight = [sends[k] and tree[k] == owner for k in range(LINE)]
        to = pick(here, [chip(way, tree[k]) if sends[k] else 0 for k in range(LINE)])
        box = pick(here, [
            LINE + SLOTS * way + children(owner, owner).index(k) if straight[k] else chip(way, owner) for k in range(LINE)
        ])
        alone = pick(here, [int(sends[k] and not children(owner, k)) for k in range(LINE)]) == 1
        adds = pick(here, [int(sends[k] and len(children(owner, k)) == 1) for k in range(LINE)]) == 1
        return to, box, alone, adds

    routed = {(way, owner): routes(way, owner) for way in range(2) for owner in range(1, LINE)}

    def step_to(way, owner):
        to, box, _, _ = routed[way, owner]
        return pltpu.make_async_remote_copy(
            src_ref=part.at[core, ORDER.index(chip(way, owner))], dst_ref=held.at[box],
            send_sem=tree_send.at[chip(way, owner)], recv_sem=tree_recv.at[box],
            device_id=(site, to * 2 + core), device_id_type=MESH,
        )

    def arrived(box):
        ref = held.at[box]
        pltpu.make_async_remote_copy(
            src_ref=ref, dst_ref=ref, send_sem=tree_send.at[0], recv_sem=tree_recv.at[box],
            device_id=twin, device_id_type=MESH,
        ).wait_recv()

    def send_leaves(owner, ways_too=(1, 0)):
        for way in ways_too:
            @pl.when(routed[way, owner][2])
            def _():
                step_to(way, owner).start()

    def send_collected(owner):
        for way in (1, 0):
            @pl.when(routed[way, owner][3])
            def _():
                box = chip(way, owner)
                arrived(box)
                part[core, ORDER.index(box)] += held[box]
                step_to(way, owner).start()

    top = wide[...].astype(jnp.bfloat16)
    rest = narrow[...].astype(jnp.bfloat16)
    tables = jnp.concatenate(
        [jnp.concatenate([top, rest], axis=1), jnp.concatenate([top, jnp.zeros_like(rest)], axis=1)], axis=0
    )

    def passed(source, target, stage, device):
        return pltpu.make_async_remote_copy(
            src_ref=source, dst_ref=target, send_sem=mom_send.at[stage], recv_sem=mom_recv.at[stage],
            device_id=device, device_id_type=MESH,
        )

    def whole(buffer, count, stage):
        ref = buffer.at[pl.ds(0, count)]
        return pltpu.make_async_remote_copy(
            src_ref=ref, dst_ref=ref, send_sem=mom_send.at[stage], recv_sem=mom_recv.at[stage],
            device_id=twin, device_id_type=MESH,
        )

    loads[0].wait()
    groups(begin, 0, 6)
    begin(96, 12)
    loads[1].wait()
    groups(finish, 0, 4)
    pl.semaphore_wait(barrier, expected)
    to_twin(0).start()
    for i, step in enumerate((2, -2)):
        signal(greet.at[i], at_z(step))
    share = project(*CUTS[0])
    finish(64, 16)
    finish(80, 16)
    finish(96, 12)
    to_twin(1).start()
    share = share + project(*CUTS[1])

    slot = 2 * height + core
    for par in range(2):
        for i in range(2):
            folded = []
            for q in range(4):
                one = share[8 * par + 4 * i + q]
                one = one + pltpu.roll(one, 4, 0)
                folded.append(one + pltpu.roll(one, 64, 1))
            pairs = [jnp.where(upper, folded[2 * j], folded[2 * j + 1]) for j in range(2)]
            own[par, 8 * i : 8 * i + 8] = jnp.where(lane < 64, pairs[0], pairs[1])

    def to_root(r, par):
        return passed(own.at[par], line.at[slot], 0, (xy, 2 * r + par))

    for r in range(ROOTS):
        @pl.when(height != r)
        def _():
            for par in range(2):
                to_root(r, par).start()

    @pl.when(root)
    def _():
        passed(own.at[1 - core], line.at[slot], 0, twin).start()
        line[slot] = own[core]

    for cut in range(2):
        from_twin(cut)
    for owner in (7, 6):
        send_leaves(owner)
    for owner in (5, 4, 3, 2, 1):
        send_leaves(owner, (0,))

    for i in range(2):
        pl.semaphore_wait(greet.at[i], 1)
    for i, step in enumerate((2, -2)):
        signal(greet.at[2 + i], at_z(step))
    for i in range(2):
        pl.semaphore_wait(greet.at[2 + i], 1)
    for owner in (7, 6):
        send_collected(owner)
    mine = pick(place, [ORDER.index(p) for p in range(LINE)])

    def take(way, n):
        box = LINE + SLOTS * way + n
        arrived(box)
        part[core, mine] += held[box]

    for way in range(2):
        @pl.when(ways[way] == LINE - 1)
        def _():
            take(way, SLOTS - 1)
    for owner in (5, 4, 3, 2, 1):
        send_leaves(owner, (1,))

    def added(buffer, first, count):
        value = buffer[first]
        for i in range(1, count):
            value = value + buffer[first + i]
        return value

    @pl.when(root)
    def _():
        whole(line, 31, 0).wait_recv()
        plane[xy] = added(line, 0, 32)
        for step in range(1, 16):
            passed(plane.at[xy], plane.at[xy], 1, at_plane(lax.rem(xy + step, 16))).start()

    for owner in (5, 4, 3, 2):
        send_collected(owner)

    def spread_out(start):
        for r in range(ROOTS):
            @pl.when(height == r)
            def _():
                for z in (8, 9, 10, 11, 12, 13, 14, 15) if r == 0 else (7, 6, 5, 4, 3, 2):
                    for c in range(2):
                        copy = passed(both.at[core], both.at[core], 2, (z // LINE * 16 + xy, z % LINE * 2 + c))
                        copy.start() if start else copy.wait_send()

    @pl.when(root)
    def _():
        whole(plane, 15, 1).wait_recv()
        both[core] = added(plane, 0, 16) * (L**-1.5)
        passed(both.at[core], both.at[core], 2, twin).start()
        spread_out(True)

    for way in range(2):
        counts = [0] + [len(children(owner, owner)) for owner in range(1, LINE)]
        counts[LINE - 1] = SLOTS - 1
        count = pick(ways[way], counts)
        for n in range(SLOTS - 1):
            @pl.when(count > n)
            def _():
                take(way, n)
    total = part[core, mine]
    imaginary = pick(mode, [int(t[0]) for t in TRACES]) == 1
    field_out[0:ROWS] = jnp.where(imaginary, 0.0, total)[0:ROWS]
    field_out[ROWS : 2 * ROWS] = jnp.where(imaginary, total, 0.0)[0:ROWS]

    @pl.when(root)
    def _():
        passed(both.at[core], both.at[core], 2, twin).wait_recv()

    @pl.when(jnp.logical_not(root))
    def _():
        whole(both, 2, 2).wait_recv()

    for par in range(2):
        value = both[par]
        turned = [value] + [pltpu.roll(value, 128 - s, 1) for s in (32, 64, 96)]
        for q in range(8):
            n = 2 * ORDER[q] + par
            first = 8 * (q // 4) + 4 * (q % 2)
            c, s = (turned[2 * (q % 4 // 2) + j][first : first + 4, 0:27] for j in range(2))
            mom_out[0, n] = s if TRACES[n][0] else c
            mom_out[1, n] = c if TRACES[n][0] else -s

    for cut in range(2):
        to_twin(cut).wait_send()
    for r in range(ROOTS):
        @pl.when(height != r)
        def _():
            for par in range(2):
                to_root(r, par).wait_send()
    for d in range(LINE):
        @pl.when(place != d)
        def _():
            ref = held.at[0]
            pltpu.make_async_remote_copy(
                src_ref=ref, dst_ref=ref, send_sem=tree_send.at[d], recv_sem=tree_recv.at[0],
                device_id=twin, device_id_type=MESH,
            ).wait_send()

    @pl.when(root)
    def _():
        passed(own.at[1 - core], line.at[slot], 0, twin).wait_send()
        whole(plane, 15, 1).wait_send()
        passed(both.at[core], both.at[core], 2, twin).wait_send()
        spread_out(False)


def deliver(field_in, mom_in, field_out, mom_out, sem):
    copies = [
        pltpu.make_async_copy(field_in, field_out, sem.at[0]),
        pltpu.make_async_copy(mom_in, mom_out, sem.at[1]),
    ]
    for copy in copies:
        copy.start()
    for copy in copies:
        copy.wait()


def shards(eigvecs, eigenvalues, block_map, momenta):
    vectors = eigvecs.transpose(0, 1, 2, 3, 5, 4, 6)

    def body(ev, *refs):
        kernel(ev.reshape(96, ROWS, 128), *refs)

    dma, vmem = pltpu.SemaphoreType.DMA, pltpu.VMEM
    anywhere = pl.BlockSpec(memory_space=pl.ANY)
    shapes = ((2 * ROWS, 128), (2, 16, 4, 27))
    field, sums = pl.pallas_call(
        body,
        out_shape=tuple(pltpu.VMEM(shape, F32) for shape in shapes),
        in_specs=[pl.BlockSpec(memory_space=pltpu.HBM)] * 4,
        out_specs=(pl.BlockSpec(memory_space=pltpu.VMEM), pl.BlockSpec(memory_space=pltpu.VMEM)),
        scratch_shapes=[
            vmem((96, ROWS, 128), jnp.bfloat16),
            vmem((16, PAD, 128), F32),
            vmem((2, 8, PAD, 128), F32),
            vmem((8, PAD, 128), F32),
            vmem((LINE + 2 * SLOTS, PAD, 128), F32),
            vmem((128, 128), F32),
            vmem((128, 128), F32),
            vmem((PAD, 128), F32),
            vmem((8, 128), jnp.int32),
            vmem((2, 16, 128), F32),
            vmem((32, 16, 128), F32),
            vmem((16, 16, 128), F32),
            vmem((2, 16, 128), F32),
            pltpu.SMEM((4,), F32),
            pltpu.SMEM((27,), jnp.int32),
            vmem((3, 27), jnp.int32),
            dma((5,)),
            dma((2,)),
            dma((2,)),
            dma((LINE,)),
            dma((LINE + 2 * SLOTS,)),
            dma((3,)),
            dma((3,)),
            pltpu.SemaphoreType.REGULAR((4,)),
        ],
        compiler_params=pltpu.CompilerParams(collective_id=0, has_side_effects=True, vmem_limit_bytes=56 * 2**20),
        name="loops",
    )(vectors, eigenvalues, block_map, momenta.T)
    field, sums = pl.pallas_call(
        deliver,
        out_shape=tuple(jax.ShapeDtypeStruct(shape, F32) for shape in shapes),
        in_specs=[pl.BlockSpec(memory_space=pltpu.VMEM)] * 2,
        out_specs=(anywhere, anywhere),
        scratch_shapes=[dma((2,))],
        name="deliver",
    )(*(pltpu.with_memory_space_constraint(a, pltpu.VMEM) for a in (field, sums)))
    field = field.reshape(2, 1, 27, 4, 128).transpose(0, 1, 3, 2, 4)
    return field, sums


def solution(mesh):
    placed = (P("mode", None, None, None, None, "site", None), P("mode"), P("site"), P())
    return jax.shard_map(
        shards,
        mesh=mesh,
        in_specs=placed,
        out_specs=(P(None, "mode", None, "site", None), P()),
        check_vma=False,
    )
```

```python
import math

import jax
import jax.numpy as jnp
import numpy as np
from jax import lax
from jax.experimental import pallas as pl
from jax.experimental.pallas import tpu as pltpu
from jax.sharding import PartitionSpec as P

MESH = pl.DeviceIdType.MESH
F32 = jnp.float32
L = 48
LINE = 8
ROWS = 108
PAD = 112
CUTS = ((0, 64), (64, 48))
ORDER = (7, 6, 0, 1, 5, 4, 3, 2)
PAIRS = tuple((s, r) for s in range(4) for r in range(s + 1, 4))
NAMES = tuple(("d", s, s) for s in range(4)) + tuple((kind, s, r) for s, r in PAIRS for kind in ("a", "b"))
ROOTS = 2

TREE = {
    7: {0: 1, 1: 7, 2: 3, 3: 7, 4: 5, 5: 7, 6: 7},
    6: {0: 1, 1: 6, 2: 3, 3: 6, 4: 5, 5: 6},
    5: {0: 1, 1: 5, 2: 3, 3: 5, 4: 5},
    4: {0: 1, 1: 4, 2: 3, 3: 4},
    3: {0: 1, 1: 3, 2: 3},
    2: {0: 1, 1: 2},
    1: {0: 1},
}
SLOTS = 4
FAR_FIRST = sorted(
    ((dy, dx) for dy in range(4) for dx in range(4) if dy or dx), key=lambda s: -min(s[0], 4 - s[0]) - min(s[1], 4 - s[1])
)


def children(owner, place):
    return sorted(k for k, to in TREE[owner].items() if to == place)


def pick(index, values):
    out = jnp.int32(values[0])
    for i in range(1, len(values)):
        if values[i] != values[0]:
            out = jnp.where(index == i, jnp.int32(values[i]), out)
    return out


def gammas():
    u = 1j
    first = np.array([[0, 0, 0, u], [0, 0, u, 0], [0, -u, 0, 0], [-u, 0, 0, 0]])
    second = np.array([[0, 0, 0, -1], [0, 0, 1, 0], [0, 1, 0, 0], [-1, 0, 0, 0]], dtype=complex)
    third = np.array([[0, 0, u, 0], [0, 0, 0, -u], [-u, 0, 0, 0], [0, u, 0, 0]])
    fourth = np.array([[0, 0, 1, 0], [0, 0, 0, 1], [1, 0, 0, 0], [0, 1, 0, 0]], dtype=complex)
    basis = [first, second, third, fourth]
    fifth = first @ second @ third @ fourth
    out = []
    for number in range(16):
        matrix = np.eye(4, dtype=complex)
        for bit in range(4):
            if number >> bit & 1:
                matrix = matrix @ basis[bit]
        out.append(matrix @ fifth)
    return out


def traces():
    out = []
    for matrix in gammas():
        terms = []
        for s in range(4):
            if matrix[s, s] != 0:
                terms.append((matrix[s, s], ("d", s, s)))
            for r in range(s + 1, 4):
                real, imag = matrix[s, r] + matrix[r, s], 1j * (matrix[s, r] - matrix[r, s])
                if real != 0:
                    terms.append((real, ("a", s, r)))
                if imag != 0:
                    terms.append((imag, ("b", s, r)))
        imaginary = all(c.real == 0 for c, _ in terms)
        values = [(c.imag if imaginary else c.real, name) for c, name in terms]
        out.append((imaginary, [(c > 0, abs(c) == 2, name) for c, name in values]))
    return out


TRACES = traces()


def cosine(index):
    turn = index - 48.0 * jnp.floor(index * (1.0 / 48.0) + 0.5)
    x = (12.0 - jnp.abs(turn)) * (math.pi / 24.0)
    y = x * x
    p = -1.0 / 39916800.0
    for c in (1.0 / 362880.0, -1.0 / 5040.0, 1.0 / 120.0, -1.0 / 6.0, 1.0):
        p = p * y + c
    return x * p


def kernel(
    ev, eig_in, bmap_in, mom_in, field_out, mom_out,
    buf, sums, part, other, held, wide, narrow, phase, lanes, own, line, plane, both, eig, bmap, mom,
    load_sem, core_send, core_recv, tree_send, tree_recv, mom_send, mom_recv, greet,
):
    site, mode = lax.axis_index("site"), lax.axis_index("mode")
    place, core = mode // 2, mode % 2
    half, xy = site // 16, site % 16
    height = half * LINE + place

    def at_z(step):
        z = lax.rem(height + step + 16, 16)
        return (z // LINE * 16 + xy, z % LINE * 2 + core)

    def at_plane(column):
        return (half * 16 + column, mode)

    def signal(sem, device):
        pl.semaphore_signal(sem, inc=1, device_id=device, device_id_type=MESH)

    twin = (site, place * 2 + 1 - core)
    loads = [
        pltpu.make_async_copy(ev.at[pl.ds(48 * m, 48)], buf.at[pl.ds(48 * m, 48)], load_sem.at[m]) for m in range(2)
    ]
    small = [
        pltpu.make_async_copy(source, target, load_sem.at[2 + i])
        for i, (source, target) in enumerate(((eig_in, eig), (bmap_in, bmap), (mom_in, mom)))
    ]
    for copy in small + loads:
        copy.start()
    barrier = pltpu.get_barrier_semaphore()
    near = (1, -1, 2, -2)
    root = height < ROOTS
    signal(barrier, twin)
    for step in near:
        signal(barrier, at_z(step))
    expected = jnp.int32(1 + len(near))
    for r in range(ROOTS):
        apart = lax.rem(height - r + 16, 16)
        expected = expected + jnp.where((apart > 2) & (apart < 14), 2, jnp.where(apart == 0, 0, 1))

    @pl.when(root)
    def _():
        for step in range(3, 14):
            signal(barrier, at_z(step))
        for step in range(1, 16):
            z = lax.rem(height + step, 16)
            signal(barrier, (z // LINE * 16 + xy, z % LINE * 2 + 1 - core))
        for step in range(1, 16):
            signal(barrier, at_plane(lax.rem(xy + step, 16)))

    expected = expected + jnp.where(root, 15, 0)

    for copy in small:
        copy.wait()
    lanes[...] = jnp.zeros((8, 128), jnp.int32)
    lanes[0:3, 0:27] = mom[...]
    spread = lanes[...].astype(F32)
    spread = spread + pltpu.roll(spread, 32, 1)
    spread = spread + pltpu.roll(spread, 64, 1)
    along = [jnp.broadcast_to(spread[i : i + 1], (8, 128)) for i in range(3)]
    lane = lax.broadcasted_iota(jnp.int32, (8, 128), 1)
    row = lax.broadcasted_iota(jnp.int32, (8, 128), 0)
    quarter = jnp.where(lane % 64 < 32, 0.0, -12.0)
    inner = along[2] * row.astype(F32) + quarter
    for i in range(16):
        values = cosine(inner + along[1] * float(i % 4) + along[0] * float(i // 4))
        top = values.astype(jnp.bfloat16).astype(F32)
        wide[8 * i : 8 * i + 8] = jnp.where(lane < 64, top, values - top)
        narrow[8 * i : 8 * i + 8] = jnp.where(lane < 64, top, 0.0)
    turn = jnp.where(lane < 64, 0.0, -12.0)
    upper = row < 4
    for i in range(14):
        one, two = bmap[2 * i], bmap[min(2 * i + 1, 26)]
        def both_rows(f):
            return jnp.where(upper, f(one), f(two)).astype(F32)
        angle = along[0] * both_rows(lambda q: 4 * (q // 72)) + along[1] * both_rows(lambda q: 4 * (q // 6 % 12))
        angle = angle + along[2] * both_rows(lambda q: 8 * (q % 6))
        phase[8 * i : 8 * i + 8] = cosine(angle + turn)
    weights = [1.0 / jnp.full((8, 128), eig[m], F32) for m in range(4)]
    for par in range(2):
        for q in range(8):
            part[par, q, 104:112] = jnp.zeros((8, 128), F32)

    def density(modes, load):
        total = {}
        for m in modes:
            inside = {}
            for c in range(3):
                real = [load(m * 24 + s * 3 + c) for s in range(4)]
                imag = [load(m * 24 + 12 + s * 3 + c) for s in range(4)]
                for key in NAMES:
                    kind, s, r = key
                    if kind == "b":
                        value = real[s] * imag[r] - imag[s] * real[r]
                    else:
                        value = real[s] * real[r] + imag[s] * imag[r]
                    inside[key] = inside[key] + value if c else value
            for key in NAMES:
                value = weights[m][0 : inside[key].shape[0]] * inside[key]
                total[key] = total[key] + value if m != modes[0] else value
        return total

    def halves(base, size):
        for first in range(0, size, 8):
            last = min(first + 8, size)
            yield first, last - first, lambda p, i=first, j=last: buf[p, pl.ds(base, size)].astype(F32)[i:j]

    def begin(base, size):
        for first, count, load in halves(base, size):
            total = density((0, 1), load)
            for i, key in enumerate(NAMES):
                sums[i, pl.ds(base + first, count)] = total[key]

    def finish(base, size):
        for first, count, load in halves(base, size):
            total = density((2, 3), load)
            for i, key in enumerate(NAMES):
                total[key] = total[key] + sums[i, pl.ds(base + first, count)]
            for q in range(8):
                for par in range(2):
                    terms = TRACES[2 * ORDER[q] + par][1]
                    value = None
                    for positive, _, name in terms:
                        if value is None:
                            value = total[name] if positive else -total[name]
                        else:
                            value = value + total[name] if positive else value - total[name]
                    if terms[0][1]:
                        value = value + value
                    part[par, q, pl.ds(base + first, count)] = value

    def project(start, size):
        rows = pl.ds(start, size)
        field = jnp.concatenate([part[par, q, rows] for par in range(2) for q in range(8)], axis=0)
        high = field.astype(jnp.bfloat16)
        low = (field - high.astype(F32)).astype(jnp.bfloat16)
        value = jnp.dot(jnp.concatenate([high, low], axis=1), tables, preferred_element_type=F32)
        value = value + pltpu.roll(value, 64, 1)
        value = (value.reshape(16, size // 8, 8, 128) * phase[rows].reshape(1, size // 8, 8, 128)).sum(axis=1)
        return value

    def groups(what, first, last):
        def body(g, carry):
            what(pl.multiple_of(g * 16, 16), 16)
            return carry
        lax.fori_loop(first, last, body, 0)

    def to_twin(cut):
        start, size = CUTS[cut]
        return pltpu.make_async_remote_copy(
            src_ref=part.at[1 - core, :, pl.ds(start, size)], dst_ref=other.at[:, pl.ds(start, size)],
            send_sem=core_send.at[cut], recv_sem=core_recv.at[cut], device_id=twin, device_id_type=MESH,
        )

    def from_twin(cut):
        to_twin(cut).wait_recv()
        start, size = CUTS[cut]
        for q in range(8):
            part[core, q, start : start + size] += other[q, start : start + size]

    ways = (place, LINE - 1 - place)

    def chip(way, k):
        return k if way == 0 else LINE - 1 - k

    def routes(way, owner):
        here, tree = ways[way], TREE[owner]
        sends = [k in tree for k in range(LINE)]
        straight = [sends[k] and tree[k] == owner for k in range(LINE)]
        to = pick(here, [chip(way, tree[k]) if sends[k] else 0 for k in range(LINE)])
        box = pick(here, [
            LINE + SLOTS * way + children(owner, owner).index(k) if straight[k] else chip(way, owner) for k in range(LINE)
        ])
        alone = pick(here, [int(sends[k] and not children(owner, k)) for k in range(LINE)]) == 1
        adds = pick(here, [int(sends[k] and len(children(owner, k)) == 1) for k in range(LINE)]) == 1
        return to, box, alone, adds

    routed = {(way, owner): routes(way, owner) for way in range(2) for owner in range(1, LINE)}

    def step_to(way, owner):
        to, box, _, _ = routed[way, owner]
        return pltpu.make_async_remote_copy(
            src_ref=part.at[core, ORDER.index(chip(way, owner))], dst_ref=held.at[box],
            send_sem=tree_send.at[chip(way, owner)], recv_sem=tree_recv.at[box],
            device_id=(site, to * 2 + core), device_id_type=MESH,
        )

    def arrived(box):
        ref = held.at[box]
        pltpu.make_async_remote_copy(
            src_ref=ref, dst_ref=ref, send_sem=tree_send.at[0], recv_sem=tree_recv.at[box],
            device_id=twin, device_id_type=MESH,
        ).wait_recv()

    def send_leaves(owner, ways_too=(1, 0)):
        for way in ways_too:
            @pl.when(routed[way, owner][2])
            def _():
                step_to(way, owner).start()

    def send_collected(owner):
        for way in (1, 0):
            @pl.when(routed[way, owner][3])
            def _():
                box = chip(way, owner)
                arrived(box)
                part[core, ORDER.index(box)] += held[box]
                step_to(way, owner).start()

    tables = jnp.concatenate([wide[...], narrow[...]], axis=0).astype(jnp.bfloat16)

    def passed(source, target, stage, device):
        return pltpu.make_async_remote_copy(
            src_ref=source, dst_ref=target, send_sem=mom_send.at[stage], recv_sem=mom_recv.at[stage],
            device_id=device, device_id_type=MESH,
        )

    def whole(buffer, count, stage):
        ref = buffer.at[pl.ds(0, count)]
        return pltpu.make_async_remote_copy(
            src_ref=ref, dst_ref=ref, send_sem=mom_send.at[stage], recv_sem=mom_recv.at[stage],
            device_id=twin, device_id_type=MESH,
        )

    loads[0].wait()
    groups(begin, 0, 6)
    begin(96, 12)
    loads[1].wait()
    groups(finish, 0, 4)
    share = project(*CUTS[0])
    finish(64, 16)
    finish(80, 16)
    finish(96, 12)
    share = share + project(*CUTS[1])

    slot = 2 * height + core
    for par in range(2):
        for i in range(2):
            folded = [share[8 * par + 4 * i + q] for q in range(4)]
            folded = [one + pltpu.roll(one, 4, 0) for one in folded]
            pairs = [jnp.where(upper, folded[2 * j], folded[2 * j + 1]) for j in range(2)]
            pairs = [one + jnp.where(lane < 32, -pltpu.roll(one, 32, 1), pltpu.roll(one, 96, 1)) for one in pairs]
            own[par, 8 * i : 8 * i + 8] = jnp.where(lane < 64, pairs[0], pltpu.roll(pairs[1], 64, 1))

    def to_root(r, par):
        return passed(own.at[par], line.at[slot], 0, (xy, 2 * r + par))

    pl.semaphore_wait(barrier, expected)
    for i, step in enumerate((2, -2)):
        signal(greet.at[i], at_z(step))
    for r in range(ROOTS):
        @pl.when(height != r)
        def _():
            for par in range(2):
                to_root(r, par).start()

    @pl.when(root)
    def _():
        passed(own.at[1 - core], line.at[slot], 0, twin).start()
        line[slot] = own[core]

    for cut in range(2):
        to_twin(cut).start()
    for cut in range(2):
        from_twin(cut)
    for owner in (7, 6):
        send_leaves(owner)
    for owner in (5, 4, 3, 2, 1):
        send_leaves(owner, (0,))

    for i in range(2):
        pl.semaphore_wait(greet.at[i], 1)
    for i, step in enumerate((2, -2)):
        signal(greet.at[2 + i], at_z(step))
    for i in range(2):
        pl.semaphore_wait(greet.at[2 + i], 1)
    for owner in (7, 6):
        send_collected(owner)
    mine = pick(place, [ORDER.index(p) for p in range(LINE)])

    def take(way, n):
        box = LINE + SLOTS * way + n
        arrived(box)
        part[core, mine] += held[box]

    for way in range(2):
        @pl.when(ways[way] == LINE - 1)
        def _():
            take(way, SLOTS - 1)
    for owner in (5, 4, 3, 2, 1):
        send_leaves(owner, (1,))

    def added(buffer, first, count):
        value = buffer[first]
        for i in range(1, count):
            value = value + buffer[first + i]
        return value

    @pl.when(root)
    def _():
        whole(line, 31, 0).wait_recv()
        plane[xy] = added(line, 0, 32)
        for dy, dx in FAR_FIRST:
            column = lax.rem(xy // 4 + dy, 4) * 4 + lax.rem(xy % 4 + dx, 4)
            passed(plane.at[xy], plane.at[xy], 1, at_plane(column)).start()

    for owner in (5, 4, 3, 2):
        send_collected(owner)

    def spread_out(start):
        for r in range(ROOTS):
            @pl.when(height == r)
            def _():
                for z in (8, 9, 10, 11, 12, 13, 14, 15) if r == 0 else (2, 3, 4, 5, 6, 7):
                    for c in range(2):
                        copy = passed(both.at[core], both.at[core], 2, (z // LINE * 16 + xy, z % LINE * 2 + c))
                        copy.start() if start else copy.wait_send()

    @pl.when(root)
    def _():
        whole(plane, 15, 1).wait_recv()
        both[core] = added(plane, 0, 16) * (L**-1.5)
        passed(both.at[core], both.at[core], 2, twin).start()
        spread_out(True)

    for way in range(2):
        counts = [0] + [len(children(owner, owner)) for owner in range(1, LINE)]
        counts[LINE - 1] = SLOTS - 1
        count = pick(ways[way], counts)
        for n in range(SLOTS - 1):
            @pl.when(count > n)
            def _():
                take(way, n)
    total = part[core, mine]
    imaginary = pick(mode, [int(t[0]) for t in TRACES]) == 1
    field_out[0:ROWS] = jnp.where(imaginary, 0.0, total)[0:ROWS]
    field_out[ROWS : 2 * ROWS] = jnp.where(imaginary, total, 0.0)[0:ROWS]

    @pl.when(root)
    def _():
        passed(both.at[core], both.at[core], 2, twin).wait_recv()

    @pl.when(jnp.logical_not(root))
    def _():
        whole(both, 2, 2).wait_recv()

    for par in range(2):
        value = both[par]
        turned = [value] + [pltpu.roll(value, 128 - s, 1) for s in (32, 64, 96)]
        for q in range(8):
            n = 2 * ORDER[q] + par
            first = 8 * (q // 4) + 4 * (q % 2)
            c, s = (turned[2 * (q % 4 // 2) + j][first : first + 4, 0:27] for j in range(2))
            mom_out[0, n] = s if TRACES[n][0] else c
            mom_out[1, n] = c if TRACES[n][0] else -s

    for cut in range(2):
        to_twin(cut).wait_send()
    for r in range(ROOTS):
        @pl.when(height != r)
        def _():
            for par in range(2):
                to_root(r, par).wait_send()
    for d in range(LINE):
        @pl.when(place != d)
        def _():
            ref = held.at[0]
            pltpu.make_async_remote_copy(
                src_ref=ref, dst_ref=ref, send_sem=tree_send.at[d], recv_sem=tree_recv.at[0],
                device_id=twin, device_id_type=MESH,
            ).wait_send()

    @pl.when(root)
    def _():
        passed(own.at[1 - core], line.at[slot], 0, twin).wait_send()
        whole(plane, 15, 1).wait_send()
        passed(both.at[core], both.at[core], 2, twin).wait_send()
        spread_out(False)


def deliver(field_in, mom_in, field_out, mom_out, sem):
    copies = [
        pltpu.make_async_copy(field_in, field_out, sem.at[0]),
        pltpu.make_async_copy(mom_in, mom_out, sem.at[1]),
    ]
    for copy in copies:
        copy.start()
    for copy in copies:
        copy.wait()


def shards(eigvecs, eigenvalues, block_map, momenta):
    vectors = eigvecs.transpose(0, 1, 2, 3, 5, 4, 6)

    def body(ev, *refs):
        kernel(ev.reshape(96, ROWS, 128), *refs)

    dma, vmem = pltpu.SemaphoreType.DMA, pltpu.VMEM
    anywhere = pl.BlockSpec(memory_space=pl.ANY)
    shapes = ((2 * ROWS, 128), (2, 16, 4, 27))
    field, sums = pl.pallas_call(
        body,
        out_shape=tuple(pltpu.VMEM(shape, F32) for shape in shapes),
        in_specs=[pl.BlockSpec(memory_space=pltpu.HBM)] * 4,
        out_specs=(pl.BlockSpec(memory_space=pltpu.VMEM), pl.BlockSpec(memory_space=pltpu.VMEM)),
        scratch_shapes=[
            vmem((96, ROWS, 128), jnp.bfloat16),
            vmem((16, PAD, 128), F32),
            vmem((2, 8, PAD, 128), F32),
            vmem((8, PAD, 128), F32),
            vmem((LINE + 2 * SLOTS, PAD, 128), F32),
            vmem((128, 128), F32),
            vmem((128, 128), F32),
            vmem((PAD, 128), F32),
            vmem((8, 128), jnp.int32),
            vmem((2, 16, 128), F32),
            vmem((32, 16, 128), F32),
            vmem((16, 16, 128), F32),
            vmem((2, 16, 128), F32),
            pltpu.SMEM((4,), F32),
            pltpu.SMEM((27,), jnp.int32),
            vmem((3, 27), jnp.int32),
            dma((5,)),
            dma((2,)),
            dma((2,)),
            dma((LINE,)),
            dma((LINE + 2 * SLOTS,)),
            dma((3,)),
            dma((3,)),
            pltpu.SemaphoreType.REGULAR((4,)),
        ],
        compiler_params=pltpu.CompilerParams(collective_id=0, has_side_effects=True, vmem_limit_bytes=56 * 2**20),
        name="loops",
    )(vectors, eigenvalues, block_map, momenta.T)
    field, sums = pl.pallas_call(
        deliver,
        out_shape=tuple(jax.ShapeDtypeStruct(shape, F32) for shape in shapes),
        in_specs=[pl.BlockSpec(memory_space=pltpu.VMEM)] * 2,
        out_specs=(anywhere, anywhere),
        scratch_shapes=[dma((2,))],
        name="deliver",
    )(*(pltpu.with_memory_space_constraint(a, pltpu.VMEM) for a in (field, sums)))
    field = field.reshape(2, 1, 27, 4, 128).transpose(0, 1, 3, 2, 4)
    return field, sums


def solution(mesh):
    placed = (P("mode", None, None, None, None, "site", None), P("mode"), P("site"), P())
    return jax.shard_map(
        shards,
        mesh=mesh,
        in_specs=placed,
        out_specs=(P(None, "mode", None, "site", None), P()),
        check_vma=False,
    )
```

```python
import math

import jax
import jax.numpy as jnp
import numpy as np
from jax import lax
from jax.experimental import pallas as pl
from jax.experimental.pallas import tpu as pltpu
from jax.sharding import PartitionSpec as P

MESH = pl.DeviceIdType.MESH
F32 = jnp.float32
L = 48
LINE = 8
ROWS = 108
PAD = 112
CUTS = ((0, 64), (64, 48))
ORDER = (7, 6, 0, 1, 5, 4, 3, 2)
PAIRS = tuple((s, r) for s in range(4) for r in range(s + 1, 4))
NAMES = tuple(("d", s, s) for s in range(4)) + tuple((kind, s, r) for s, r in PAIRS for kind in ("a", "b"))
ROOTS = 2

TREE = {
    7: {0: 1, 1: 7, 2: 3, 3: 7, 4: 5, 5: 7, 6: 7},
    6: {0: 1, 1: 6, 2: 3, 3: 6, 4: 5, 5: 6},
    5: {0: 1, 1: 5, 2: 3, 3: 5, 4: 5},
    4: {0: 1, 1: 4, 2: 3, 3: 4},
    3: {0: 1, 1: 3, 2: 3},
    2: {0: 1, 1: 2},
    1: {0: 1},
}
SLOTS = 4
FAR_FIRST = sorted(
    ((dy, dx) for dy in range(4) for dx in range(4) if dy or dx), key=lambda s: -min(s[0], 4 - s[0]) - min(s[1], 4 - s[1])
)


def children(owner, place):
    return sorted(k for k, to in TREE[owner].items() if to == place)


def pick(index, values):
    out = jnp.int32(values[0])
    for i in range(1, len(values)):
        if values[i] != values[0]:
            out = jnp.where(index == i, jnp.int32(values[i]), out)
    return out


def gammas():
    u = 1j
    first = np.array([[0, 0, 0, u], [0, 0, u, 0], [0, -u, 0, 0], [-u, 0, 0, 0]])
    second = np.array([[0, 0, 0, -1], [0, 0, 1, 0], [0, 1, 0, 0], [-1, 0, 0, 0]], dtype=complex)
    third = np.array([[0, 0, u, 0], [0, 0, 0, -u], [-u, 0, 0, 0], [0, u, 0, 0]])
    fourth = np.array([[0, 0, 1, 0], [0, 0, 0, 1], [1, 0, 0, 0], [0, 1, 0, 0]], dtype=complex)
    basis = [first, second, third, fourth]
    fifth = first @ second @ third @ fourth
    out = []
    for number in range(16):
        matrix = np.eye(4, dtype=complex)
        for bit in range(4):
            if number >> bit & 1:
                matrix = matrix @ basis[bit]
        out.append(matrix @ fifth)
    return out


def traces():
    out = []
    for matrix in gammas():
        terms = []
        for s in range(4):
            if matrix[s, s] != 0:
                terms.append((matrix[s, s], ("d", s, s)))
            for r in range(s + 1, 4):
                real, imag = matrix[s, r] + matrix[r, s], 1j * (matrix[s, r] - matrix[r, s])
                if real != 0:
                    terms.append((real, ("a", s, r)))
                if imag != 0:
                    terms.append((imag, ("b", s, r)))
        imaginary = all(c.real == 0 for c, _ in terms)
        values = [(c.imag if imaginary else c.real, name) for c, name in terms]
        out.append((imaginary, [(c > 0, abs(c) == 2, name) for c, name in values]))
    return out


TRACES = traces()


def cosine(index):
    turn = index - 48.0 * jnp.floor(index * (1.0 / 48.0) + 0.5)
    x = (12.0 - jnp.abs(turn)) * (math.pi / 24.0)
    y = x * x
    p = -1.0 / 39916800.0
    for c in (1.0 / 362880.0, -1.0 / 5040.0, 1.0 / 120.0, -1.0 / 6.0, 1.0):
        p = p * y + c
    return x * p


def kernel(
    ev, eig_in, bmap_in, mom_in, field_out, mom_out,
    buf, sums, part, other, held, wide, narrow, phase, lanes, own, line, plane, both, eig, bmap, mom,
    load_sem, core_send, core_recv, tree_send, tree_recv, mom_send, mom_recv, greet,
):
    site, mode = lax.axis_index("site"), lax.axis_index("mode")
    place, core = mode // 2, mode % 2
    half, xy = site // 16, site % 16
    height = half * LINE + place

    def at_z(step):
        z = lax.rem(height + step + 16, 16)
        return (z // LINE * 16 + xy, z % LINE * 2 + core)

    def at_plane(column):
        return (half * 16 + column, mode)

    def signal(sem, device):
        pl.semaphore_signal(sem, inc=1, device_id=device, device_id_type=MESH)

    twin = (site, place * 2 + 1 - core)
    loads = [
        pltpu.make_async_copy(ev.at[pl.ds(48 * m, 48)], buf.at[pl.ds(48 * m, 48)], load_sem.at[m]) for m in range(2)
    ]
    small = [
        pltpu.make_async_copy(source, target, load_sem.at[2 + i])
        for i, (source, target) in enumerate(((eig_in, eig), (bmap_in, bmap), (mom_in, mom)))
    ]
    for copy in small + loads:
        copy.start()
    barrier = pltpu.get_barrier_semaphore()
    near = (1, -1, 2, -2)
    root = height < ROOTS
    signal(barrier, twin)
    for step in near:
        signal(barrier, at_z(step))
    expected = jnp.int32(1 + len(near))
    for r in range(ROOTS):
        apart = lax.rem(height - r + 16, 16)
        expected = expected + jnp.where((apart > 2) & (apart < 14), 2, jnp.where(apart == 0, 0, 1))

    @pl.when(root)
    def _():
        for step in range(3, 14):
            signal(barrier, at_z(step))
        for step in range(1, 16):
            z = lax.rem(height + step, 16)
            signal(barrier, (z // LINE * 16 + xy, z % LINE * 2 + 1 - core))
        for step in range(1, 16):
            signal(barrier, at_plane(lax.rem(xy + step, 16)))

    expected = expected + jnp.where(root, 15, 0)

    for copy in small:
        copy.wait()
    lanes[...] = jnp.zeros((8, 128), jnp.int32)
    lanes[0:3, 0:27] = mom[...]
    spread = lanes[...].astype(F32)
    spread = spread + pltpu.roll(spread, 32, 1)
    spread = spread + pltpu.roll(spread, 64, 1)
    along = [jnp.broadcast_to(spread[i : i + 1], (8, 128)) for i in range(3)]
    lane = lax.broadcasted_iota(jnp.int32, (8, 128), 1)
    row = lax.broadcasted_iota(jnp.int32, (8, 128), 0)
    quarter = jnp.where(lane % 64 < 32, 0.0, -12.0)
    inner = along[2] * row.astype(F32) + quarter
    for i in range(16):
        values = cosine(inner + along[1] * float(i % 4) + along[0] * float(i // 4))
        top = values.astype(jnp.bfloat16).astype(F32)
        wide[8 * i : 8 * i + 8] = jnp.where(lane < 64, top, values - top)
        narrow[8 * i : 8 * i + 8] = jnp.where(lane < 64, top, 0.0)
    turn = jnp.where(lane < 64, 0.0, -12.0)
    upper = row < 4
    for i in range(14):
        one, two = bmap[2 * i], bmap[min(2 * i + 1, 26)]
        def both_rows(f):
            return jnp.where(upper, f(one), f(two)).astype(F32)
        angle = along[0] * both_rows(lambda q: 4 * (q // 72)) + along[1] * both_rows(lambda q: 4 * (q // 6 % 12))
        angle = angle + along[2] * both_rows(lambda q: 8 * (q % 6))
        phase[8 * i : 8 * i + 8] = cosine(angle + turn)
    weights = [1.0 / jnp.full((8, 128), eig[m], F32) for m in range(4)]
    for par in range(2):
        for q in range(8):
            part[par, q, 104:112] = jnp.zeros((8, 128), F32)

    def density(modes, load):
        total = {}
        for m in modes:
            inside = {}
            for c in range(3):
                real = [load(m * 24 + s * 3 + c) for s in range(4)]
                imag = [load(m * 24 + 12 + s * 3 + c) for s in range(4)]
                for key in NAMES:
                    kind, s, r = key
                    if kind == "b":
                        value = real[s] * imag[r] - imag[s] * real[r]
                    else:
                        value = real[s] * real[r] + imag[s] * imag[r]
                    inside[key] = inside[key] + value if c else value
            for key in NAMES:
                value = weights[m][0 : inside[key].shape[0]] * inside[key]
                total[key] = total[key] + value if m != modes[0] else value
        return total

    def halves(base, size):
        for first in range(0, size, 8):
            last = min(first + 8, size)
            yield first, last - first, lambda p, i=first, j=last: buf[p, pl.ds(base, size)].astype(F32)[i:j]

    def begin(base, size):
        for first, count, load in halves(base, size):
            total = density((0, 1), load)
            for i, key in enumerate(NAMES):
                sums[i, pl.ds(base + first, count)] = total[key]

    def finish(base, size):
        for first, count, load in halves(base, size):
            total = density((2, 3), load)
            for i, key in enumerate(NAMES):
                total[key] = total[key] + sums[i, pl.ds(base + first, count)]
            for q in range(8):
                for par in range(2):
                    terms = TRACES[2 * ORDER[q] + par][1]
                    value = None
                    for positive, _, name in terms:
                        if value is None:
                            value = total[name] if positive else -total[name]
                        else:
                            value = value + total[name] if positive else value - total[name]
                    if terms[0][1]:
                        value = value + value
                    part[par, q, pl.ds(base + first, count)] = value

    def project(start, size):
        rows = pl.ds(start, size)
        field = jnp.concatenate([part[par, q, rows] for par in range(2) for q in range(8)], axis=0)
        high = field.astype(jnp.bfloat16)
        low = (field - high.astype(F32)).astype(jnp.bfloat16)
        value = jnp.dot(jnp.concatenate([high, low], axis=1), tables, preferred_element_type=F32)
        value = value + pltpu.roll(value, 64, 1)
        value = (value.reshape(16, size // 8, 8, 128) * phase[rows].reshape(1, size // 8, 8, 128)).sum(axis=1)
        return value

    def groups(what, first, last):
        def body(g, carry):
            what(pl.multiple_of(g * 16, 16), 16)
            return carry
        lax.fori_loop(first, last, body, 0)

    to_twin = pltpu.make_async_remote_copy(
        src_ref=part.at[1 - core], dst_ref=other, send_sem=core_send.at[0], recv_sem=core_recv.at[0],
        device_id=twin, device_id_type=MESH,
    )

    ways = (place, LINE - 1 - place)

    def chip(way, k):
        return k if way == 0 else LINE - 1 - k

    def routes(way, owner):
        here, tree = ways[way], TREE[owner]
        sends = [k in tree for k in range(LINE)]
        straight = [sends[k] and tree[k] == owner for k in range(LINE)]
        to = pick(here, [chip(way, tree[k]) if sends[k] else 0 for k in range(LINE)])
        box = pick(here, [
            LINE + SLOTS * way + children(owner, owner).index(k) if straight[k] else chip(way, owner) for k in range(LINE)
        ])
        alone = pick(here, [int(sends[k] and not children(owner, k)) for k in range(LINE)]) == 1
        adds = pick(here, [int(sends[k] and len(children(owner, k)) == 1) for k in range(LINE)]) == 1
        return to, box, alone, adds

    routed = {(way, owner): routes(way, owner) for way in range(2) for owner in range(1, LINE)}

    def step_to(way, owner):
        to, box, _, _ = routed[way, owner]
        return pltpu.make_async_remote_copy(
            src_ref=part.at[core, ORDER.index(chip(way, owner))], dst_ref=held.at[box],
            send_sem=tree_send.at[chip(way, owner)], recv_sem=tree_recv.at[box],
            device_id=(site, to * 2 + core), device_id_type=MESH,
        )

    def arrived(box):
        ref = held.at[box]
        pltpu.make_async_remote_copy(
            src_ref=ref, dst_ref=ref, send_sem=tree_send.at[0], recv_sem=tree_recv.at[box],
            device_id=twin, device_id_type=MESH,
        ).wait_recv()

    def send_leaves(owner, ways_too=(1, 0)):
        for way in ways_too:
            @pl.when(routed[way, owner][2])
            def _():
                step_to(way, owner).start()

    def send_collected(owner):
        for way in (1, 0):
            @pl.when(routed[way, owner][3])
            def _():
                box = chip(way, owner)
                arrived(box)
                part[core, ORDER.index(box)] += held[box]
                step_to(way, owner).start()

    tables = jnp.concatenate([wide[...], narrow[...]], axis=0).astype(jnp.bfloat16)

    def passed(source, target, stage, device):
        return pltpu.make_async_remote_copy(
            src_ref=source, dst_ref=target, send_sem=mom_send.at[stage], recv_sem=mom_recv.at[stage],
            device_id=device, device_id_type=MESH,
        )

    def whole(buffer, count, stage):
        ref = buffer.at[pl.ds(0, count)]
        return pltpu.make_async_remote_copy(
            src_ref=ref, dst_ref=ref, send_sem=mom_send.at[stage], recv_sem=mom_recv.at[stage],
            device_id=twin, device_id_type=MESH,
        )

    loads[0].wait()
    groups(begin, 0, 6)
    begin(96, 12)
    loads[1].wait()
    groups(finish, 0, 4)
    share = project(*CUTS[0])
    finish(64, 16)
    finish(80, 16)
    finish(96, 12)
    share = share + project(*CUTS[1])

    slot = 2 * height + core
    for par in range(2):
        for i in range(2):
            folded = [share[8 * par + 4 * i + q] for q in range(4)]
            folded = [one + pltpu.roll(one, 4, 0) for one in folded]
            pairs = [jnp.where(upper, folded[2 * j], folded[2 * j + 1]) for j in range(2)]
            pairs = [one + jnp.where(lane < 32, -pltpu.roll(one, 32, 1), pltpu.roll(one, 96, 1)) for one in pairs]
            own[par, 8 * i : 8 * i + 8] = jnp.where(lane < 64, pairs[0], pltpu.roll(pairs[1], 64, 1))

    def to_root(r, par):
        return passed(own.at[par], line.at[slot], 0, (xy, 2 * r + par))

    pl.semaphore_wait(barrier, expected)
    for i, step in enumerate((2, -2)):
        signal(greet.at[i], at_z(step))
    for r in range(ROOTS):
        @pl.when(height != r)
        def _():
            for par in range(2):
                to_root(r, par).start()

    @pl.when(root)
    def _():
        passed(own.at[1 - core], line.at[slot], 0, twin).start()
        line[slot] = own[core]

    to_twin.start()
    to_twin.wait_recv()
    for q in range(8):
        part[core, q] += other[q]
    for owner in (7, 6):
        send_leaves(owner)
    for owner in (5, 4, 3, 2, 1):
        send_leaves(owner, (0,))

    for i in range(2):
        pl.semaphore_wait(greet.at[i], 1)
    for i, step in enumerate((2, -2)):
        signal(greet.at[2 + i], at_z(step))
    for i in range(2):
        pl.semaphore_wait(greet.at[2 + i], 1)
    for owner in (7, 6):
        send_collected(owner)
    mine = pick(place, [ORDER.index(p) for p in range(LINE)])

    def take(way, n):
        box = LINE + SLOTS * way + n
        arrived(box)
        part[core, mine] += held[box]

    for way in range(2):
        @pl.when(ways[way] == LINE - 1)
        def _():
            take(way, SLOTS - 1)
    for owner in (5, 4, 3, 2, 1):
        send_leaves(owner, (1,))

    def added(buffer, first, count):
        value = buffer[first]
        for i in range(1, count):
            value = value + buffer[first + i]
        return value

    @pl.when(root)
    def _():
        whole(line, 31, 0).wait_recv()
        plane[xy] = added(line, 0, 32)
        for dy, dx in FAR_FIRST:
            column = lax.rem(xy // 4 + dy, 4) * 4 + lax.rem(xy % 4 + dx, 4)
            passed(plane.at[xy], plane.at[xy], 1, at_plane(column)).start()

    for owner in (5, 4, 3, 2):
        send_collected(owner)

    def spread_out(start):
        for r in range(ROOTS):
            @pl.when(height == r)
            def _():
                for z in (8, 9, 10, 11, 12, 13, 14, 15) if r == 0 else (2, 3, 4, 5, 6, 7):
                    for c in range(2):
                        copy = passed(both.at[core], both.at[core], 2, (z // LINE * 16 + xy, z % LINE * 2 + c))
                        copy.start() if start else copy.wait_send()

    @pl.when(root)
    def _():
        whole(plane, 15, 1).wait_recv()
        both[core] = added(plane, 0, 16) * (L**-1.5)
        passed(both.at[core], both.at[core], 2, twin).start()
        spread_out(True)

    for way in range(2):
        counts = [0] + [len(children(owner, owner)) for owner in range(1, LINE)]
        counts[LINE - 1] = SLOTS - 1
        count = pick(ways[way], counts)
        for n in range(SLOTS - 1):
            @pl.when(count > n)
            def _():
                take(way, n)
    total = part[core, mine]
    imaginary = pick(mode, [int(t[0]) for t in TRACES]) == 1
    field_out[0:ROWS] = jnp.where(imaginary, 0.0, total)[0:ROWS]
    field_out[ROWS : 2 * ROWS] = jnp.where(imaginary, total, 0.0)[0:ROWS]

    def laid_out(par):
        value = both[par]
        turned = [value] + [pltpu.roll(value, 128 - s, 1) for s in (32, 64, 96)]
        for q in range(8):
            n = 2 * ORDER[q] + par
            first = 8 * (q // 4) + 4 * (q % 2)
            c, s = (turned[2 * (q % 4 // 2) + j][first : first + 4, 0:27] for j in range(2))
            mom_out[0, n] = s if TRACES[n][0] else c
            mom_out[1, n] = c if TRACES[n][0] else -s

    @pl.when(root)
    def _():
        for par in range(2):
            @pl.when(core == par)
            def _():
                laid_out(par)
        passed(both.at[core], both.at[core], 2, twin).wait_recv()
        for par in range(2):
            @pl.when(core != par)
            def _():
                laid_out(par)

    @pl.when(jnp.logical_not(root))
    def _():
        whole(both, 2, 2).wait_recv()
        for par in range(2):
            laid_out(par)

    to_twin.wait_send()
    for r in range(ROOTS):
        @pl.when(height != r)
        def _():
            for par in range(2):
                to_root(r, par).wait_send()
    for d in range(LINE):
        @pl.when(place != d)
        def _():
            ref = held.at[0]
            pltpu.make_async_remote_copy(
                src_ref=ref, dst_ref=ref, send_sem=tree_send.at[d], recv_sem=tree_recv.at[0],
                device_id=twin, device_id_type=MESH,
            ).wait_send()

    @pl.when(root)
    def _():
        passed(own.at[1 - core], line.at[slot], 0, twin).wait_send()
        whole(plane, 15, 1).wait_send()
        passed(both.at[core], both.at[core], 2, twin).wait_send()
        spread_out(False)


def deliver(field_in, mom_in, field_out, mom_out, sem):
    copies = [
        pltpu.make_async_copy(field_in, field_out, sem.at[0]),
        pltpu.make_async_copy(mom_in, mom_out, sem.at[1]),
    ]
    for copy in copies:
        copy.start()
    for copy in copies:
        copy.wait()


def shards(eigvecs, eigenvalues, block_map, momenta):
    vectors = eigvecs.transpose(0, 1, 2, 3, 5, 4, 6)

    def body(ev, *refs):
        kernel(ev.reshape(96, ROWS, 128), *refs)

    dma, vmem = pltpu.SemaphoreType.DMA, pltpu.VMEM
    anywhere = pl.BlockSpec(memory_space=pl.ANY)
    shapes = ((2 * ROWS, 128), (2, 16, 4, 27))
    field, sums = pl.pallas_call(
        body,
        out_shape=tuple(pltpu.VMEM(shape, F32) for shape in shapes),
        in_specs=[pl.BlockSpec(memory_space=pltpu.HBM)] * 4,
        out_specs=(pl.BlockSpec(memory_space=pltpu.VMEM), pl.BlockSpec(memory_space=pltpu.VMEM)),
        scratch_shapes=[
            vmem((96, ROWS, 128), jnp.bfloat16),
            vmem((16, PAD, 128), F32),
            vmem((2, 8, PAD, 128), F32),
            vmem((8, PAD, 128), F32),
            vmem((LINE + 2 * SLOTS, PAD, 128), F32),
            vmem((128, 128), F32),
            vmem((128, 128), F32),
            vmem((PAD, 128), F32),
            vmem((8, 128), jnp.int32),
            vmem((2, 16, 128), F32),
            vmem((32, 16, 128), F32),
            vmem((16, 16, 128), F32),
            vmem((2, 16, 128), F32),
            pltpu.SMEM((4,), F32),
            pltpu.SMEM((27,), jnp.int32),
            vmem((3, 27), jnp.int32),
            dma((5,)),
            dma((1,)),
            dma((1,)),
            dma((LINE,)),
            dma((LINE + 2 * SLOTS,)),
            dma((3,)),
            dma((3,)),
            pltpu.SemaphoreType.REGULAR((4,)),
        ],
        compiler_params=pltpu.CompilerParams(collective_id=0, has_side_effects=True, vmem_limit_bytes=56 * 2**20),
        name="loops",
    )(vectors, eigenvalues, block_map, momenta.T)
    field, sums = pl.pallas_call(
        deliver,
        out_shape=tuple(jax.ShapeDtypeStruct(shape, F32) for shape in shapes),
        in_specs=[pl.BlockSpec(memory_space=pltpu.VMEM)] * 2,
        out_specs=(anywhere, anywhere),
        scratch_shapes=[dma((2,))],
        name="deliver",
    )(*(pltpu.with_memory_space_constraint(a, pltpu.VMEM) for a in (field, sums)))
    field = field.reshape(2, 1, 27, 4, 128).transpose(0, 1, 3, 2, 4)
    return field, sums


def solution(mesh):
    placed = (P("mode", None, None, None, None, "site", None), P("mode"), P("site"), P())
    return jax.shard_map(
        shards,
        mesh=mesh,
        in_specs=placed,
        out_specs=(P(None, "mode", None, "site", None), P()),
        check_vma=False,
    )
```
